32 devices in a mesh: pulse: 4 (over y, x), gate: 8 (over z, core).
Axes of the slice: x: 2, y: 2, z: 4, core: 2. Of those that a mesh axis runs over, the one named last changes fastest.
Arguments:
- echoes: bfloat16 [2, 8, 2048, 4096], P(None, None, 'pulse', 'gate'), may hold values from -6 to 6
- replica: bfloat16 [2, 256], replicated, may hold values from -4 to 4
- beam_weights: float32 [2, 2, 8, 2048], P(None, None, None, 'pulse'), may hold values from -1.5 to 1.5
- track_doppler: int32 [8192], P(('pulse', 'gate')), may hold values from 0 to 2047, as said below
- track_gate: int32 [8192], P(('pulse', 'gate')), may hold values from 0 to 4095, as said below
- track_owner: int32 [8192], P(('pulse', 'gate')), may hold values from 0 to 31, as said below
Outputs:
- track_tiles: float32 [20480, 1024], P(('pulse', 'gate'))
The draws below stay inside these ranges and needn't reach their ends.
Inputs may be any that keep to these rules, and one draw needn't show every extreme that they name: `track_doppler`: row k lies in Doppler block (k // 256) // 8: its bin is in that block of 512 bins. `track_gate`: row k lies in range block (k // 256) % 8: its gate is in that block of 512 gates. `track_owner`: within each aligned block of 256 rows no owner appears more than 20 times, and in every draw some owner appears exactly 20 times in every block.
All inputs are finite; a program needn't handle non-finite values.
Results may differ from the reference program's by a relative error of at most 0.015.
Values may be sent and summed in bfloat16 or wider, within the bound.
No kernel may reach another device: no remote copies, remote signals or barrier semaphores. Data moves between devices by JAX's collectives and lax.ppermute only.
A program may use at most 704 MiB of HBM per device.

```python
import math
import jax
import jax.numpy as jnp
from jax import lax

CH = 8
NPULSE = 2048
NGATE = 4096
CHIRP = 256
BEAMS = 2
TILE = 16
TRK_DEV = 256
DOP_DEV = 512
GATE_DEV = 512
RANGE_BLOCKS = 8
OWNERS = 32
CAP = 20
TRACKS = 8192


def draw_track_doppler(key, part):
    row_index = jnp.arange(TRACKS, dtype=jnp.int32)
    block_index = row_index // TRK_DEV // RANGE_BLOCKS
    offsets = jax.random.randint(jax.random.fold_in(key, 1), (TRACKS,), 0, DOP_DEV, dtype=jnp.int32)
    return block_index * DOP_DEV + offsets


def draw_track_gate(key, part):
    row_index = jnp.arange(TRACKS, dtype=jnp.int32)
    block_index = row_index // TRK_DEV % RANGE_BLOCKS
    offsets = jax.random.randint(jax.random.fold_in(key, 2), (TRACKS,), 0, GATE_DEV, dtype=jnp.int32)
    return block_index * GATE_DEV + offsets


def draw_track_owner(key, part):
    slot_total = OWNERS * CAP
    hot_owners = jax.random.permutation(jax.random.fold_in(key, 31), OWNERS)[:2]
    slot_owner = jnp.arange(slot_total, dtype=jnp.int32) // CAP
    is_hot = jnp.any(slot_owner[:, None] == hot_owners[None, :], axis=1)

    def one_block(holder):
        slot_order = jax.random.permutation(jax.random.fold_in(jax.random.fold_in(key, 37), holder), slot_total)
        cold_flag = jnp.where(is_hot[slot_order], 0, 1).astype(jnp.int32)
        chosen = slot_order[jnp.argsort(cold_flag, stable=True)][:TRK_DEV]
        shuffled = jax.random.permutation(jax.random.fold_in(jax.random.fold_in(key, 41), holder), chosen)
        return (shuffled // CAP).astype(jnp.int32)
    return jax.vmap(one_block)(jnp.arange(OWNERS, dtype=jnp.int32)).reshape(-1)


def level_of(own_key, extent, split, least, top_value):
    factor_of = 1.0
    for position, blocks in split:
        draws = jax.random.uniform(jax.random.fold_in(jax.random.fold_in(own_key, 6), position), (blocks,), jnp.float32, least / len(split), top_value / len(split))
        factor_of = factor_of * jnp.repeat(jnp.exp(draws), extent[position] // blocks).reshape((-1,) + (1,) * (len(extent) - 1 - position))
    return factor_of


def centred(own_key, shape, spread, reach, shards=(), kind=jnp.bfloat16):
    entries = spread * jax.random.normal(own_key, shape, jnp.float32)
    if shards:
        entries = entries * level_of(own_key, shape, shards, -0.22, 0.18)
    return jnp.clip(entries, -reach, reach).astype(kind)


def setup_inputs(seed: int = 0) -> dict:
    streams_of = jax.random.split(jax.random.key(seed), 7)
    return {
        "echoes": centred(streams_of[0], (2, CH, NPULSE, NGATE), 1.0, 6.0, ((2, 4), (3, 8))),
        "replica": centred(streams_of[1], (2, CHIRP), 1.0, 4.0),
        "beam_weights": centred(streams_of[2], (2, BEAMS, CH, NPULSE), (2 * CH) ** -0.5, 1.5, ((3, 4),), jnp.float32),
        "track_doppler": draw_track_doppler(jax.random.fold_in(streams_of[6], 71), 0),
        "track_gate": draw_track_gate(jax.random.fold_in(streams_of[6], 71), 0),
        "track_owner": draw_track_owner(jax.random.fold_in(streams_of[6], 71), 0),
    }


def reference(echoes, replica, beam_weights, track_doppler, track_gate, track_owner):
    range_scale = 1.0 / math.sqrt(2.0 * CHIRP)
    total_len = NGATE + CHIRP
    replica_wave = replica[0].astype(jnp.float32) + 1j * replica[1].astype(jnp.float32)
    replica_hat = jnp.conj(jnp.fft.fft(replica_wave, n=total_len))

    def one_channel(channel):
        echo_wave = channel[0].astype(jnp.float32) + 1j * channel[1].astype(jnp.float32)
        correlated = jnp.fft.ifft(jnp.fft.fft(echo_wave, n=total_len, axis=1) * replica_hat[None, :], axis=1)
        correlated = correlated[:, :NGATE] * range_scale
        comp_real = jnp.real(correlated).astype(jnp.bfloat16)
        comp_imag = jnp.imag(correlated).astype(jnp.bfloat16)
        comp_wave = comp_real.astype(jnp.float32) + 1j * comp_imag.astype(jnp.float32)
        spectral = jnp.fft.fft(comp_wave, axis=0) / math.sqrt(NPULSE)
        return jnp.stack([jnp.real(spectral).astype(jnp.bfloat16), jnp.imag(spectral).astype(jnp.bfloat16)])
    spectra = lax.map(one_channel, jnp.moveaxis(echoes, 1, 0))
    beam_real = jnp.zeros((BEAMS, NPULSE, NGATE), jnp.float32)
    beam_imag = jnp.zeros((BEAMS, NPULSE, NGATE), jnp.float32)
    for channel in range(CH):
        spec_real = spectra[channel, 0].astype(jnp.float32)[None]
        spec_imag = spectra[channel, 1].astype(jnp.float32)[None]
        weight_real = beam_weights[0, :, channel, :][:, :, None]
        weight_imag = beam_weights[1, :, channel, :][:, :, None]
        beam_real = beam_real + weight_real * spec_real - weight_imag * spec_imag
        beam_imag = beam_imag + weight_real * spec_imag + weight_imag * spec_real
    beams = jnp.stack([beam_real, beam_imag])
    half_tile = TILE // 2
    framed = jnp.pad(beams, ((0, 0), (0, 0), (half_tile, half_tile), (half_tile, half_tile)))
    zero_index = jnp.zeros((), jnp.int32)

    def cut_tile(doppler_bin, range_gate):
        starts = (zero_index, zero_index, doppler_bin.astype(jnp.int32), range_gate.astype(jnp.int32))
        return lax.dynamic_slice(framed, starts, (2, BEAMS, TILE, TILE)).reshape(-1)
    tile_rows = jax.vmap(cut_tile)(track_doppler.astype(jnp.int32), track_gate.astype(jnp.int32))
    owners = track_owner.astype(jnp.int32).reshape(OWNERS, TRK_DEV)
    owner_match = (owners[:, :, None] == jnp.arange(OWNERS, dtype=jnp.int32)[None, None, :]).astype(jnp.int32)
    running = jnp.cumsum(owner_match, axis=1, dtype=jnp.int32)
    slot_rank = (lax.optimization_barrier(jnp.sum(running * owner_match, axis=2, dtype=jnp.int32)) - 1).astype(jnp.int32)
    holder = jnp.broadcast_to(jnp.arange(OWNERS, dtype=jnp.int32)[:, None], owners.shape)
    row_index = ((owners * OWNERS + holder) * CAP + slot_rank).reshape(-1).astype(jnp.int32)
    result = jnp.zeros((OWNERS * OWNERS * CAP, tile_rows.shape[1]), jnp.float32)
    return result.at[row_index].set(tile_rows)
```

```python
import functools
import math

import jax
import jax.numpy as jnp
import ml_dtypes
import numpy as np
from jax import lax
from jax.experimental import pallas as pl
from jax.experimental.pallas import tpu as pltpu
from jax.sharding import PartitionSpec as P

TILE = 16
HALF = TILE // 2
LANES = 128
F32 = jnp.float32
BF16 = jnp.bfloat16
VMEM_LIMIT = 63 * 2**20
SMALL_COST = pl.CostEstimate(flops=2**20, bytes_accessed=2**16, transcendentals=0)


def passed_along(value, axis, steps):
    count = lax.axis_size(axis)
    leading, last = (max(0, -steps), min(count, count - steps))
    return lax.ppermute(value, axis, [(source, source + steps) for source in range(leading, last)])


def pulse_table(bins, depth):
    angle = 2.0 * np.pi * (np.outer(np.arange(bins), np.arange(depth)) % bins) / bins
    cos_part, sin_part = np.cos(angle), np.sin(angle)
    table = np.stack(
        [np.concatenate([cos_part, sin_part], 1), np.concatenate([-sin_part, cos_part], 1)]
    )
    table = table.reshape(2, bins // 8, 8, 2 * depth).transpose(1, 0, 2, 3)
    return table.reshape(2 * bins, 2 * depth).astype(ml_dtypes.bfloat16)


def weights_body(ranks, me_ref, *rest):
    parts, rest = rest[:ranks], rest[ranks:]
    cos_ref, sin_ref, select_ref, spread_ref, out_ref, line_ref = rest[:4] + rest[-2:]
    bins = parts[0].shape[1]
    span = out_ref.shape[0] * 8
    lanes = cos_ref.shape[1]
    me = me_ref[0]
    step = pl.program_id(0)

    @pl.when(step == 0)
    def _():
        line_ref[:HALF, :] = jnp.zeros((HALF, line_ref.shape[1]), F32)
        line_ref[HALF + ranks * bins :, :] = jnp.zeros((HALF, line_ref.shape[1]), F32)
        for slot in range(ranks):
            first = pl.multiple_of((slot ^ me) * bins + HALF, 8)
            line_ref[pl.ds(first, bins), :] = parts[slot][...].T

    base_cos, base_sin = cos_ref[...], sin_ref[...]
    lane_id = lax.broadcasted_iota(jnp.int32, (span, lanes), 1)
    phase = lane_id // 2 % ranks
    first_part = lane_id % 2 == 0
    offset = lax.broadcasted_iota(jnp.int32, (span, lanes), 0) + step * span + (ranks * 8 - HALF)
    lines = []
    for slot in range(ranks):
        block = slot ^ me
        rows = line_ref[pl.ds(pl.multiple_of(block * bins + step * span, 8), span), :]
        high = rows.astype(BF16)
        low = (rows - high.astype(F32)).astype(BF16)
        wide = jnp.dot(high, select_ref[...], preferred_element_type=F32) + jnp.dot(
            low, select_ref[...], preferred_element_type=F32
        )
        turn = (me * offset + block * phase) & (ranks - 1)
        turn_cos = jnp.ones(turn.shape, F32)
        turn_sin = jnp.zeros(turn.shape, F32)
        for value in range(1, ranks):
            angle = 2 * math.pi * value / ranks
            turn_cos = jnp.where(turn == value, round(math.cos(angle), 12), turn_cos)
            turn_sin = jnp.where(turn == value, round(math.sin(angle), 12), turn_sin)
        cos_part = turn_cos * base_cos - turn_sin * base_sin
        sin_part = turn_sin * base_cos + turn_cos * base_sin
        own = jnp.where(first_part, cos_part, sin_part)
        other = jnp.where(first_part, sin_part, -cos_part)
        real, imag = wide[:, :lanes], wide[:, lanes:]
        out_real = (real * own + imag * other).reshape(span // 8, 8, lanes)
        out_imag = (imag * own - real * other).reshape(span // 8, 8, lanes)
        both = jnp.concatenate([out_real, out_imag], axis=1).reshape(span * 2, lanes)
        lines.append(both.astype(BF16))
    product = jnp.dot(
        jnp.concatenate(lines, axis=0), spread_ref[...], preferred_element_type=F32
    )
    row_id = lax.broadcasted_iota(jnp.int32, product.shape, 0) % 8
    diagonal = row_id == lax.broadcasted_iota(jnp.int32, product.shape, 1) % 8
    product = jnp.where(diagonal, product, 0.0).astype(BF16)
    product = product.reshape(ranks, span // 8, 16, product.shape[1])
    depth = out_ref.shape[3]
    for beam in range(product.shape[3] // depth):
        for slot in range(ranks):
            out_ref[:, beam * ranks + slot] = product[
                slot, :, :, beam * depth : (beam + 1) * depth
            ]


def divisor_up_to(value, limit):
    return max(step for step in range(1, limit + 1) if value % step == 0)


def combining_weights(beam_weights, pulse_len, extra, before):
    _, beams, channels, bins = beam_weights.shape
    ranks = lax.axis_size("pulse")
    me = lax.axis_index("pulse")
    total = bins * ranks
    rows = bins + TILE
    count = 2 * beams * channels
    flat = jnp.concatenate([beam_weights.reshape(count, bins), extra])
    parts = [flat] + [
        lax.ppermute(flat, "pulse", [(rank, rank ^ slot) for rank in range(ranks)])
        for slot in range(1, ranks)
    ]
    small = channels * ranks * 2
    column = np.arange(small)
    phase = column // 2 % ranks
    angle = 2.0 * np.pi * (np.outer(np.arange(rows) - HALF, phase) % total) / total
    scale = 1.0 / math.sqrt(total * 2.0 * pulse_len)
    base_cos = np.tile(np.cos(angle) * scale, (1, beams)).astype(np.float32)
    base_sin = np.tile(np.sin(angle) * scale, (1, beams)).astype(np.float32)
    lanes = beams * small
    source = np.arange(count)[:, None]
    target = np.arange(2 * lanes)[None, :]
    wanted = target // small * channels + target % small // (2 * ranks)
    select = (source == wanted).astype(ml_dtypes.bfloat16)
    spread = (np.arange(lanes * 8)[None, :] // 8 == np.arange(lanes)[:, None]).astype(
        ml_dtypes.bfloat16
    )
    groups = rows // 8
    per = divisor_up_to(groups, 11)
    scalar = pl.BlockSpec(memory_space=pltpu.SMEM)
    table = pl.pallas_call(
        functools.partial(weights_body, ranks),
        grid=(groups // per,),
        out_shape=jax.ShapeDtypeStruct((groups, beams * ranks, 16, small * 8), BF16),
        in_specs=[scalar]
        + [pl.BlockSpec((count, bins), lambda i: (0, 0))] * ranks
        + [
            pl.BlockSpec((per * 8, lanes), lambda i: (i, 0)),
            pl.BlockSpec((per * 8, lanes), lambda i: (i, 0)),
            pl.BlockSpec(select.shape, lambda i: (0, 0)),
            pl.BlockSpec(spread.shape, lambda i: (0, 0)),
        ]
        + [pl.BlockSpec(memory_space=pl.ANY)] * len(before),
        out_specs=pl.BlockSpec((per, beams * ranks, 16, small * 8), lambda i: (i, 0, 0, 0)),
        scratch_shapes=[pltpu.VMEM((total + TILE, count), F32)],
        compiler_params=pltpu.CompilerParams(vmem_limit_bytes=VMEM_LIMIT),
        cost_estimate=SMALL_COST,
        name="combining_weights",
    )(me.reshape(1), *parts, base_cos, base_sin, select, spread, *before)
    return table, [part[count:] for part in parts]


def slot_kinds(ranks):
    whole_slots = [slot for slot in range(ranks) if slot & (slot - 1) == 0]
    return whole_slots, [slot for slot in range(ranks) if slot not in whole_slots]


def partial_beams_body(ranks, beams, edges, echo_ref, table_ref, weight_hbm, *rest):
    outs, (wide_ref, taken_ref, stage_ref, weight_ref, weight_sem) = rest[:-5], rest[-5:]
    whole_slots, cut_slots = slot_kinds(ranks)
    count = len(whole_slots)
    outs = outs[-(count + 2 + len(edges)) :]
    far_ref, edge_refs, flag_ref = outs[count], outs[count + 1 : -1], outs[-1]
    flag_ref[...] = jnp.ones(flag_ref.shape, F32)
    _, channels, pulses, width = echo_ref.shape
    depth = pulses // ranks
    groups = table_ref.shape[0] // 16
    columns = width // LANES
    fetch = pltpu.make_async_copy(weight_hbm, weight_ref, weight_sem)
    fetch.start()

    def deinterleave(channel, side):
        for part in range(2):
            wide = echo_ref[part, channel].astype(F32)
            for column in range(columns):
                wide_ref[side, part, column] = wide[:, column * LANES : (column + 1) * LANES]
        for phase in range(ranks):
            here = pl.ds(phase, depth, stride=ranks)
            for part in range(2):
                for column in range(columns):
                    taken_ref[
                        side,
                        phase,
                        part * depth : (part + 1) * depth,
                        column * LANES : (column + 1) * LANES,
                    ] = wide_ref[side, part, column, here, :].astype(BF16)

    def transform(channel, side):
        for phase in range(ranks):
            product = jnp.dot(
                table_ref[...], taken_ref[side, phase], preferred_element_type=F32
            )
            stage_ref[:, channel * ranks + phase] = product.astype(BF16).reshape(groups, 16, width)

    deinterleave(0, 0)

    def two_channels(step, carry):
        first = step * 2
        deinterleave(first + 1, 1)
        transform(first, 0)
        deinterleave(lax.min(first + 2, channels - 1), 0)
        transform(first + 1, 1)
        return carry

    lax.fori_loop(0, channels // 2, two_channels, 0)
    fetch.wait()

    _, pairs, _, inner = weight_ref.shape
    lines = pairs * 2
    steps = weight_ref.shape[0] // 2
    per = divisor_up_to(steps, 4)

    def combine(turn, carry):
        for within in range(per):
            step = turn * per + within
            halves = []
            for half in range(2):
                group = step * 2 + half
                source = lax.rem(group + groups - 1, groups)
                data = stage_ref[source].reshape(inner, width)
                weight = weight_ref[group].reshape(lines * 8, inner)
                product = jnp.dot(weight, data, preferred_element_type=F32)
                halves.append(product.reshape(lines, 8, width))
            both = jnp.concatenate(halves, axis=1).astype(BF16)
            here = pl.ds(pl.multiple_of(step * 16, 16), 16)
            for line in range(lines):
                beam, slot, part = line // (2 * ranks), line // 2 % ranks, line % 2
                value = both[line]
                for tile in range(columns):
                    piece = value[:, tile * LANES : (tile + 1) * LANES]
                    lanes = slice(part * LANES, (part + 1) * LANES)
                    if slot in whole_slots:
                        outs[whole_slots.index(slot)][beam, tile, here, lanes] = piece
                        continue
                    entry = cut_slots.index(slot) * beams + beam
                    far_ref[entry, tile, here, lanes] = piece
                    for edge, edge_ref in zip(edges, edge_refs):
                        if edge == tile:
                            edge_ref[entry, 0, here, lanes] = piece
        return carry

    lax.fori_loop(0, steps // per, combine, 0)


def partial_beams(echoes, table, weights, chunk, width, edges, before=()):
    _, channels, pulses, _ = echoes.shape
    ranks = lax.axis_size("pulse")
    beams = weights.shape[1] // ranks
    rows = weights.shape[0] * 8
    groups = table.shape[0] // 16
    whole_slots, cut_slots = slot_kinds(ranks)
    far = len(cut_slots) * beams
    tiles = width // LANES
    outs = [jax.ShapeDtypeStruct((beams, tiles, rows, 2 * LANES), BF16)] * len(whole_slots)
    outs += [jax.ShapeDtypeStruct((far, tiles, rows, 2 * LANES), BF16)]
    outs += [jax.ShapeDtypeStruct((far, 1, rows, 2 * LANES), BF16)] * len(edges)
    outs += [jax.ShapeDtypeStruct((8, LANES), F32)]
    whole = pl.BlockSpec(memory_space=pltpu.VMEM)
    anywhere = pl.BlockSpec(memory_space=pl.ANY)
    result = pl.pallas_call(
        functools.partial(partial_beams_body, ranks, beams, edges),
        grid=(1,),
        out_shape=outs,
        in_specs=[
            pl.BlockSpec((2, channels, pulses, width), lambda i: (0, 0, 0, chunk)),
            whole,
            anywhere,
        ]
        + [anywhere] * len(before),
        out_specs=[whole] * len(outs),
        scratch_shapes=[
            pltpu.VMEM((2, 2, width // LANES, pulses, LANES), F32),
            pltpu.VMEM((2, ranks, 2 * pulses // ranks, width), BF16),
            pltpu.VMEM((groups, channels * ranks, 16, width), BF16),
            pltpu.VMEM(weights.shape, BF16),
            pltpu.SemaphoreType.DMA,
        ],
        compiler_params=pltpu.CompilerParams(vmem_limit_bytes=VMEM_LIMIT),
        cost_estimate=SMALL_COST,
        name="partial_beams",
    )(echoes, table, weights, *before)
    count = len(whole_slots)
    return result[:count], result[count], result[count + 1 : -1], result[-1]


def summed_body(terms, edges, *refs):
    ins, outs = refs[:terms], refs[-1 - len(edges) :]
    total = ins[0][...].astype(F32)
    for term in ins[1:]:
        total += term[...].astype(F32)
    total = total.astype(BF16)
    outs[0][...] = total
    for edge, edge_ref in zip(edges, outs[1:]):
        edge_ref[0, 0] = total[0, edge]


def summed_block(terms, edges, before=()):
    beams, tiles, rows, lanes = terms[0].shape
    block = pl.BlockSpec((1, tiles, rows, lanes), lambda i: (i, 0, 0, 0))
    single = pl.BlockSpec((1, 1, rows, lanes), lambda i: (i, 0, 0, 0))
    return pl.pallas_call(
        functools.partial(summed_body, len(terms), edges),
        grid=(beams,),
        out_shape=[jax.ShapeDtypeStruct(terms[0].shape, BF16)]
        + [jax.ShapeDtypeStruct((beams, 1, rows, lanes), BF16)] * len(edges),
        in_specs=[block] * len(terms) + [pl.BlockSpec(memory_space=pl.ANY)] * len(before),
        out_specs=[block] + [single] * len(edges),
        compiler_params=pltpu.CompilerParams(vmem_limit_bytes=VMEM_LIMIT),
        cost_estimate=SMALL_COST,
        name="summed_block",
    )(*terms, *before)


def toeplitz_body(replica_ref, before_ref, out_ref):
    chirp = replica_ref.shape[1]
    span = chirp + LANES
    padded = jnp.concatenate(
        [replica_ref[...].astype(F32), jnp.zeros((2, LANES), F32)], axis=1
    )
    taps = []
    for part in range(2):
        rows = jnp.broadcast_to(padded[part : part + 1], (LANES, span))
        taps.append(pltpu.roll(rows, 0, 1, stride=1, stride_axis=0).T)
    real, imag = (tap.astype(BF16) for tap in taps)
    split = LANES // 2
    low, high = slice(0, split), slice(split, LANES)
    for part, (own, other) in enumerate(((real, -imag), (imag, real))):
        columns = jnp.concatenate(
            [own[:, low], other[:, low], other[:, high], own[:, high]], axis=1
        )
        for tile in range(span // LANES):
            first = (2 * tile + part) * LANES
            out_ref[first : first + LANES, :] = columns[tile * LANES : (tile + 1) * LANES]


def toeplitz_taps(replica, before):
    return pl.pallas_call(
        toeplitz_body,
        out_shape=jax.ShapeDtypeStruct((2 * (replica.shape[1] + LANES), 2 * LANES), BF16),
        in_specs=[pl.BlockSpec(memory_space=pltpu.VMEM), pl.BlockSpec(memory_space=pl.ANY)],
        cost_estimate=SMALL_COST,
        name="toeplitz_taps",
    )(replica, before)


def tiles_body(tracks, place_ref, flag_ref, taps_ref, repeat_ref, gather_ref, *rest):
    pieces, (out_ref, line_ref, cut_ref) = rest[:-3], rest[-3:]
    entry = pl.program_id(0)
    rows = pieces[0].shape[2]
    span = taps_ref.shape[0] // (2 * LANES)
    columns = [(piece, tile) for piece in pieces for tile in range(piece.shape[1])]
    for block in range(len(columns) - span + 1):
        window = [piece[0, tile] for piece, tile in columns[block : block + span]]
        product = jnp.dot(
            jnp.concatenate(window, axis=1), taps_ref[...], preferred_element_type=F32
        )
        if block == 0:
            product = jnp.where(flag_ref[:1, :1] == 0.0, 0.0, product)
        line_ref[2 * block * rows : (2 * block + 1) * rows, :] = product[:, :LANES]
        line_ref[(2 * block + 1) * rows : (2 * block + 2) * rows, :] = product[:, LANES:]

    lane_id = lax.broadcasted_iota(jnp.int32, (TILE, LANES), 1) % (LANES // 2)
    batch = 16

    def cut(step, carry):
        values = []
        for within in range(batch):
            track = step * batch + within
            row = place_ref[0, entry, track]
            low = line_ref[pl.ds(row, TILE), :]
            high = line_ref[pl.ds(row + rows, TILE), :]
            values.append(jnp.where(lane_id >= place_ref[1, entry, track], low, high))
        values = [
            pltpu.roll(value, place_ref[2, entry, step * batch + within], 1)
            for within, value in enumerate(values)
        ]
        here = pl.ds(pl.multiple_of(step * batch * TILE, batch * TILE), batch * TILE)
        cut_ref[here, :] = jnp.concatenate(values, axis=0).astype(BF16)
        return carry

    lax.fori_loop(0, tracks // batch, cut, 0)

    group = 2 * LANES
    many = divisor_up_to(tracks * TILE // group, 4) * group
    row_id = lax.broadcasted_iota(jnp.int32, (many, group), 0) % 8
    wanted = row_id == lax.broadcasted_iota(jnp.int32, (many, group), 1) % LANES // TILE
    for start in range(0, tracks * TILE, many):
        repeated = jnp.dot(
            cut_ref[start : start + many, :], repeat_ref[...], preferred_element_type=F32
        )
        masked = jnp.where(wanted, repeated, 0.0).astype(BF16)
        for first in range(0, many, group):
            value = jnp.dot(
                gather_ref[...], masked[first : first + group], preferred_element_type=F32
            )
            here = (start + first) // 8
            out_ref[0, here : here + group // 8, :] = value.astype(BF16)


def slots_body(terms, slot_ref, *rest):
    parts, (out_ref, total_ref, sorted_ref) = rest[:terms], rest[-3:]
    total = parts[0][0].astype(F32)
    for part in parts[1:]:
        total += part[0].astype(F32)
    for part in range(2):
        total_ref[part] = total[:, part * LANES : (part + 1) * LANES]
    sorted_ref[...] = jnp.zeros(sorted_ref.shape, F32)

    def move(track, carry):
        target = pl.ds(slot_ref[track] * 2, 2)
        sorted_ref[:, target, :] = total_ref[:, pl.ds(track * 2, 2), :]
        return carry

    lax.fori_loop(0, slot_ref.shape[0], move, 0, unroll=8)
    for part in range(2):
        out_ref[:, part * LANES : (part + 1) * LANES] = sorted_ref[part].astype(BF16)


def slotted(terms, slots, slot_total):
    count, lanes = terms[0][0].shape[1:]
    return pl.pallas_call(
        functools.partial(slots_body, len(terms)),
        grid=(1,),
        out_shape=jax.ShapeDtypeStruct((slot_total * 2, lanes), BF16),
        in_specs=[pl.BlockSpec(memory_space=pltpu.SMEM)]
        + [
            pl.BlockSpec((1, count, lanes), lambda i, entry=entry: (entry, 0, 0))
            for _, entry in terms
        ],
        out_specs=pl.BlockSpec((slot_total * 2, lanes), lambda i: (0, 0)),
        scratch_shapes=[
            pltpu.VMEM((2, count, LANES), F32),
            pltpu.VMEM((2, slot_total * 2, LANES), F32),
        ],
        compiler_params=pltpu.CompilerParams(vmem_limit_bytes=VMEM_LIMIT),
        cost_estimate=SMALL_COST,
        name="slotted_tiles",
    )(slots, *[term for term, _ in terms])


def cut_places(bins, gates, rows):
    first = gates + (LANES - HALF)
    half = LANES // 2
    return jnp.stack([first // half * rows + bins, first % half, (LANES - first % LANES) % LANES])


def beam_tiles(taps, pieces, places, flag, gate_len):
    _, entries, tracks = places.shape
    rows = pieces[0][0].shape[2]
    scalar = pl.BlockSpec(memory_space=pltpu.SMEM)
    blocks = gate_len // LANES + 2
    group = 2 * LANES
    column = np.arange(group)[None, :]
    repeat = np.arange(LANES)[:, None] == column // LANES * (LANES // 2) + column % TILE
    repeat = repeat.astype(ml_dtypes.bfloat16)
    gather = np.arange(group // 8)[:, None] == np.arange(group)[None, :] // 8
    gather = gather.astype(ml_dtypes.bfloat16)
    return pl.pallas_call(
        functools.partial(tiles_body, tracks),
        grid=(entries,),
        out_shape=jax.ShapeDtypeStruct((entries, tracks * 2, group), BF16),
        in_specs=[
            scalar,
            pl.BlockSpec(flag.shape, lambda i: (0, 0)),
            pl.BlockSpec(taps.shape, lambda i: (0, 0)),
            pl.BlockSpec(repeat.shape, lambda i: (0, 0)),
            pl.BlockSpec(gather.shape, lambda i: (0, 0)),
        ]
        + [
            pl.BlockSpec((1,) + piece.shape[1:], lambda i, offset=offset: (i + offset, 0, 0, 0))
            for piece, offset in pieces
        ],
        out_specs=pl.BlockSpec((1, tracks * 2, group), lambda i: (i, 0, 0)),
        scratch_shapes=[
            pltpu.VMEM((2 * blocks * rows, LANES), F32),
            pltpu.VMEM((tracks * TILE, LANES), BF16),
        ],
        compiler_params=pltpu.CompilerParams(vmem_limit_bytes=VMEM_LIMIT),
        cost_estimate=SMALL_COST,
        name="beam_tiles",
    )(places, flag, taps, repeat, gather, *[piece for piece, _ in pieces])


def finish_body(*refs):
    parts, out_ref, wide_ref = refs[:-2], refs[-2], refs[-1]
    rows = out_ref.shape[0]
    for beam, part in enumerate(parts):
        for side in range(2):
            wide_ref[...] = part[:, side * LANES : (side + 1) * LANES].astype(F32)
            for half in range(2):
                column = ((side * len(parts) + beam) * 2 + half) * LANES
                out_ref[:, column : column + LANES] = wide_ref[pl.ds(half, rows, stride=2), :]


def finished(parts, rows):
    whole = pl.BlockSpec(memory_space=pltpu.VMEM)
    return pl.pallas_call(
        finish_body,
        out_shape=jax.ShapeDtypeStruct((rows, len(parts) * 4 * LANES), F32),
        in_specs=[whole] * len(parts),
        out_specs=whole,
        scratch_shapes=[pltpu.VMEM((rows * 2, LANES), F32)],
        compiler_params=pltpu.CompilerParams(vmem_limit_bytes=32 * 2**20),
        cost_estimate=SMALL_COST,
        name="finished_tiles",
    )(*parts)


def local(echoes, replica, beam_weights, track_doppler, track_gate, track_owner):
    gate_len = echoes.shape[3]
    chirp = replica.shape[1]
    _, beams, _, bins = beam_weights.shape
    ranks = lax.axis_size("pulse")
    owners = ranks * lax.axis_size("gate")
    table = pulse_table(bins, echoes.shape[2] // ranks)

    track_count = track_owner.shape[0]
    capacity = max(2, 5 * track_count // (2 * owners))
    owner_match = (
        track_owner[:, None] == jnp.arange(owners, dtype=jnp.int32)[None, :]
    ).astype(jnp.int32)
    running = jnp.cumsum(owner_match, axis=0, dtype=jnp.int32)
    slot_rank = jnp.sum(running * owner_match, axis=1, dtype=jnp.int32) - 1
    slots = track_owner * capacity + slot_rank
    place = jnp.stack([track_doppler % bins, track_gate % gate_len])

    def exchanged(value, slot):
        return lax.ppermute(value, "pulse", [(rank, rank ^ slot) for rank in range(ranks)])

    whole_slots, cut_slots = slot_kinds(ranks)

    width = gate_len // 2
    last_tile = width // LANES - 1
    spare_chunk, spare_steps = chirp % gate_len // width, chirp // gate_len + 1
    halo_chunks = [(position // gate_len + 1, position % gate_len // width) for position in range(0, chirp, width)]
    edges = [[], [last_tile]]
    edges[spare_chunk] = [0] + edges[spare_chunk]

    extra = jnp.pad(place.astype(F32), ((0, 6), (0, bins - place.shape[1])))
    rows = bins + TILE
    track_count = place.shape[1]
    place = cut_places(place[0], place[1], rows)[:, None]
    weights, extras = combining_weights(beam_weights, chirp, extra, [place])
    far_places = [extras[slot][:2, :track_count].astype(jnp.int32) for slot in cut_slots]
    far_places = jnp.stack(
        [cut_places(item[0], item[1], rows) for item in far_places for _ in range(beams)], axis=1
    )
    first_blocks, far, far_edges, flag = partial_beams(echoes, table, weights, 0, width, edges[0])
    fars, ends = [far], [far_edges]
    flag = passed_along(flag, "gate", 1)
    second_blocks, far, far_edges, ones = partial_beams(
        echoes, table, weights, 1, width, edges[1], before=[flag, far_places]
    )
    taps = toeplitz_taps(replica, ones)
    fars, ends = fars + [far], ends + [far_edges]

    def with_halo(full, spare, left):
        before = passed_along(left, "gate", 1)
        after = [passed_along(full[chunk], "gate", -steps) for steps, chunk in halo_chunks]
        return [before] + full + after + [passed_along(spare, "gate", -spare_steps)]

    def neighbours(blocks):
        return [blocks[0]] + [
            exchanged(blocks[kind], whole_slots[kind]) for kind in range(1, len(whole_slots))
        ]

    first = summed_block(neighbours(first_blocks), edges[0])
    far_pieces = with_halo(fars, ends[spare_chunk][0], ends[1][-1])
    far_tiles = beam_tiles(
        taps, [(piece, 0) for piece in far_pieces], far_places, flag, gate_len
    )
    arrived = [
        exchanged(far_tiles[kind * beams : (kind + 1) * beams], slot)
        for kind, slot in enumerate(cut_slots)
    ]
    second = summed_block(neighbours(second_blocks), edges[1], before=[far_tiles])
    own_pieces = with_halo([first[0], second[0]], [first, second][spare_chunk][1], second[-1])
    results = []
    for beam in range(beams):
        tiles = beam_tiles(
            taps, [(piece, beam) for piece in own_pieces], place, flag, gate_len
        )
        tiles = slotted(
            [(tiles, 0)] + [(item, beam) for item in arrived], slots, owners * capacity
        )
        sent = lax.all_to_all(
            tiles.reshape(owners, capacity * 2, 2 * LANES),
            ("pulse", "gate"),
            split_axis=0,
            concat_axis=0,
            tiled=True,
        )
        results.append(sent.reshape(owners * capacity * 2, 2 * LANES))
    return finished(results, owners * capacity)


def solution(mesh):
    return jax.shard_map(
        local,
        mesh=mesh,
        in_specs=(
            P(None, None, "pulse", "gate"),
            P(),
            P(None, None, None, "pulse"),
            P(("pulse", "gate")),
            P(("pulse", "gate")),
            P(("pulse", "gate")),
        ),
        out_specs=P(("pulse", "gate"), None),
        check_vma=False,
    )
```

```python
import functools
import math

import jax
import jax.numpy as jnp
import ml_dtypes
import numpy as np
from jax import lax
from jax.experimental import pallas as pl
from jax.experimental.pallas import tpu as pltpu
from jax.sharding import PartitionSpec as P

TILE = 16
HALF = TILE // 2
LANES = 128
F32 = jnp.float32
BF16 = jnp.bfloat16
VMEM_LIMIT = 63 * 2**20
SMALL_COST = pl.CostEstimate(flops=2**20, bytes_accessed=2**16, transcendentals=0)


def passed_along(value, axis, steps):
    count = lax.axis_size(axis)
    leading, last = (max(0, -steps), min(count, count - steps))
    return lax.ppermute(value, axis, [(source, source + steps) for source in range(leading, last)])


def pulse_table(bins, depth):
    angle = 2.0 * np.pi * (np.outer(np.arange(bins), np.arange(depth)) % bins) / bins
    cos_part, sin_part = np.cos(angle), np.sin(angle)
    table = np.stack(
        [np.concatenate([cos_part, sin_part], 1), np.concatenate([-sin_part, cos_part], 1)]
    )
    table = table.reshape(2, bins // 8, 8, 2 * depth).transpose(1, 0, 2, 3)
    return table.reshape(2 * bins, 2 * depth).astype(ml_dtypes.bfloat16)


def gather_lines(me, parts, line_ref):
    count, bins = line_ref.shape[1], parts[0].shape[1]
    ends = jnp.zeros((HALF, count), F32)
    line_ref[:HALF, :] = ends
    line_ref[HALF + len(parts) * bins :, :] = ends
    for slot, part in enumerate(parts):
        first = pl.multiple_of((slot ^ me) * bins + HALF, 8)
        line_ref[pl.ds(first, bins), :] = part[:count, :].T


def quarter_turns(turn, ranks):
    cos_part = jnp.ones(turn.shape, F32)
    sin_part = jnp.zeros(turn.shape, F32)
    for value in range(1, ranks):
        angle = 2 * math.pi * value / ranks
        cos_part = jnp.where(turn == value, round(math.cos(angle), 12), cos_part)
        sin_part = jnp.where(turn == value, round(math.sin(angle), 12), sin_part)
    return cos_part, sin_part


def turn_tables(ranks, me, cos_ref, sin_ref, turned_ref):
    rows, lanes = cos_ref.shape
    offset = lax.broadcasted_iota(jnp.int32, (rows, lanes), 0) + (ranks * 8 - HALF)
    turn_cos, turn_sin = quarter_turns((me * offset) & (ranks - 1), ranks)
    base_cos, base_sin = cos_ref[...], sin_ref[...]
    turned_ref[0] = turn_cos * base_cos - turn_sin * base_sin
    turned_ref[1] = turn_sin * base_cos + turn_cos * base_sin


def fill_weights(ranks, bins, slot, me, line_ref, turned_ref, select_ref, weight_ref):
    groups, pairs, _, depth = weight_ref.shape
    per = divisor_up_to(groups, 11)
    span = per * 8
    lanes = turned_ref.shape[2]
    lane_id = lax.broadcasted_iota(jnp.int32, (8, lanes), 1)
    block = slot ^ me
    slot_cos, slot_sin = quarter_turns((block * (lane_id // 2 % ranks)) & (ranks - 1), ranks)
    first_part = lane_id[:1] % 2 == 0
    slot_cos, slot_sin = slot_cos[:1], slot_sin[:1]
    own_cos = jnp.where(first_part, slot_cos, slot_sin)
    own_sin = jnp.where(first_part, -slot_sin, slot_cos)
    cells = (span * 2, LANES)
    column = lax.broadcasted_iota(jnp.int32, cells, 1)
    diagonal = lax.broadcasted_iota(jnp.int32, cells, 0) % 8 == column % 8
    source_lane = column // 8
    for step in range(groups // per):
        here = slice(step * span, (step + 1) * span)
        rows = line_ref[pl.ds(pl.multiple_of(block * bins + step * span, 8), span), :]
        high = rows.astype(BF16)
        low = (rows - high.astype(F32)).astype(BF16)
        wide = jnp.dot(high, select_ref[...], preferred_element_type=F32) + jnp.dot(
            low, select_ref[...], preferred_element_type=F32
        )
        base_cos, base_sin = turned_ref[0, here, :], turned_ref[1, here, :]
        own = base_cos * own_cos + base_sin * own_sin
        other = base_sin * own_cos - base_cos * own_sin
        real, imag = wide[:, :lanes], wide[:, lanes:]
        out_real = (real * own + imag * other).reshape(per, 8, lanes)
        out_imag = (imag * own - real * other).reshape(per, 8, lanes)
        both = jnp.concatenate([out_real, out_imag], axis=1).reshape(span * 2, lanes)
        for first in range(0, lanes * 8, LANES):
            source = first // 8 // LANES * LANES
            wide = jnp.take_along_axis(
                both[:, source : source + LANES],
                source_lane + (first // 8 - source),
                axis=1,
                mode="promise_in_bounds",
            )
            wide = jnp.where(diagonal, wide, 0.0).astype(BF16).reshape(per, 16, LANES)
            lane = first % depth
            weight_ref[
                step * per : (step + 1) * per,
                first // depth * ranks + slot,
                :,
                lane : lane + LANES,
            ] = wide


def divisor_up_to(value, limit):
    return max(step for step in range(1, limit + 1) if value % step == 0)


def weight_tables(beam_weights, pulse_len):
    _, beams, channels, bins = beam_weights.shape
    ranks = lax.axis_size("pulse")
    total = bins * ranks
    count = 2 * beams * channels
    flat = beam_weights.reshape(count, bins)
    parts = [flat] + [
        lax.ppermute(flat, "pulse", [(rank, rank ^ slot) for rank in range(ranks)])
        for slot in range(1, ranks)
    ]
    small = channels * ranks * 2
    phase = np.arange(small) // 2 % ranks
    angle = 2.0 * np.pi * (np.outer(np.arange(bins + TILE) - HALF, phase) % total) / total
    scale = 1.0 / math.sqrt(total * 2.0 * pulse_len)
    base_cos = np.tile(np.cos(angle) * scale, (1, beams)).astype(np.float32)
    base_sin = np.tile(np.sin(angle) * scale, (1, beams)).astype(np.float32)
    target = np.arange(2 * beams * small)[None, :]
    wanted = target // small * channels + target % small // (2 * ranks)
    select = (np.arange(count)[:, None] == wanted).astype(ml_dtypes.bfloat16)
    me = lax.axis_index("pulse").reshape(1)
    return [me] + parts + [base_cos, base_sin, select]


def slot_kinds(ranks):
    whole_slots = [slot for slot in range(ranks) if slot & (slot - 1) == 0]
    return whole_slots, [slot for slot in range(ranks) if slot not in whole_slots]


def partial_beams_body(ranks, beams, edges, tables, before, echo_ref, table_ref, *rest):
    sources, rest = rest[: max(tables, 1)], rest[max(tables, 1) + before :]
    outs, (wide_ref, taken_ref, stage_ref, weight_ref, weight_sem) = rest[:-7], rest[-7:-2]
    line_ref, turned_ref = rest[-2:]
    whole_slots, cut_slots = slot_kinds(ranks)
    count = len(whole_slots)
    far_ref, edge_refs, flag_ref = outs[count], outs[count + 1 : count + 1 + len(edges)], outs[count + 1 + len(edges)]
    flag_ref[...] = jnp.ones(flag_ref.shape, F32)
    _, channels, pulses, width = echo_ref.shape
    depth = pulses // ranks
    groups = table_ref.shape[0] // 16
    columns = width // LANES
    turns = channels // 2
    if tables:
        me = sources[0][0]
        bins = sources[1].shape[1]
        gather_lines(me, sources[1 : 1 + ranks], line_ref)
        turn_tables(ranks, me, *sources[1 + ranks : 3 + ranks], turned_ref)

        def weights_of(slot):
            fill_weights(ranks, bins, slot, me, line_ref, turned_ref, sources[-1], weight_ref)

        if ranks % turns:
            lax.fori_loop(0, ranks, lambda slot, carry: (weights_of(slot), carry)[1], 0)
    else:
        fetch = pltpu.make_async_copy(sources[0], weight_ref, weight_sem)
        fetch.start()

    def deinterleave(channel, side):
        for part in range(2):
            wide = echo_ref[part, channel].astype(F32)
            for column in range(columns):
                wide_ref[side, part, column] = wide[:, column * LANES : (column + 1) * LANES]
        for phase in range(ranks):
            here = pl.ds(phase, depth, stride=ranks)
            for part in range(2):
                for column in range(columns):
                    taken_ref[
                        side,
                        phase,
                        part * depth : (part + 1) * depth,
                        column * LANES : (column + 1) * LANES,
                    ] = wide_ref[side, part, column, here, :].astype(BF16)

    def transform(channel, side):
        for phase in range(ranks):
            product = jnp.dot(
                table_ref[...], taken_ref[side, phase], preferred_element_type=F32
            )
            stage_ref[:, channel * ranks + phase] = product.astype(BF16).reshape(groups, 16, width)

    deinterleave(0, 0)

    def two_channels(step, carry):
        first = step * 2
        deinterleave(first + 1, 1)
        transform(first, 0)
        deinterleave(lax.min(first + 2, channels - 1), 0)
        transform(first + 1, 1)
        if tables and ranks % turns == 0:
            for within in range(ranks // turns):
                weights_of(step * (ranks // turns) + within)
        return carry

    lax.fori_loop(0, turns, two_channels, 0)
    if tables:
        keep = pltpu.make_async_copy(weight_ref, outs[-1], weight_sem)
        keep.start()
    else:
        fetch.wait()

    _, pairs, _, inner = weight_ref.shape
    lines = pairs * 2
    steps = weight_ref.shape[0] // 2
    per = divisor_up_to(steps, 4)

    def combine(turn, carry):
        for within in range(per):
            step = turn * per + within
            halves = []
            for half in range(2):
                group = step * 2 + half
                source = lax.rem(group + groups - 1, groups)
                data = stage_ref[source].reshape(inner, width)
                weight = weight_ref[group].reshape(lines * 8, inner)
                product = jnp.dot(weight, data, preferred_element_type=F32)
                halves.append(product.reshape(lines, 8, width))
            both = jnp.concatenate(halves, axis=1).astype(BF16)
            here = pl.ds(pl.multiple_of(step * 16, 16), 16)
            for line in range(lines):
                beam, slot, part = line // (2 * ranks), line // 2 % ranks, line % 2
                value = both[line]
                for tile in range(columns):
                    piece = value[:, tile * LANES : (tile + 1) * LANES]
                    lanes = slice(part * LANES, (part + 1) * LANES)
                    if slot in whole_slots:
                        outs[whole_slots.index(slot)][beam, tile, here, lanes] = piece
                        continue
                    entry = cut_slots.index(slot) * beams + beam
                    far_ref[entry, tile, here, lanes] = piece
                    for edge, edge_ref in zip(edges, edge_refs):
                        if edge == tile:
                            edge_ref[entry, 0, here, lanes] = piece
        return carry

    lax.fori_loop(0, steps // per, combine, 0)
    if tables:
        keep.wait()


def partial_beams(echoes, table, sources, beams, chunk, width, edges, before=()):
    _, channels, pulses, _ = echoes.shape
    ranks = lax.axis_size("pulse")
    groups = table.shape[0] // 16
    rows = groups * 8 + TILE
    whole_slots, cut_slots = slot_kinds(ranks)
    far = len(cut_slots) * beams
    tiles = width // LANES
    tables = len(sources) if len(sources) > 1 else 0
    weights = jax.ShapeDtypeStruct((rows // 8, beams * ranks, 16, channels * ranks * 16), BF16)
    outs = [jax.ShapeDtypeStruct((beams, tiles, rows, 2 * LANES), BF16)] * len(whole_slots)
    outs += [jax.ShapeDtypeStruct((far, tiles, rows, 2 * LANES), BF16)]
    outs += [jax.ShapeDtypeStruct((far, 1, rows, 2 * LANES), BF16)] * len(edges)
    outs += [jax.ShapeDtypeStruct((8, LANES), F32)]
    whole = pl.BlockSpec(memory_space=pltpu.VMEM)
    anywhere = pl.BlockSpec(memory_space=pl.ANY)
    if tables:
        source_specs = [pl.BlockSpec(memory_space=pltpu.SMEM)] + [
            pl.BlockSpec(item.shape, lambda i: (0, 0)) for item in sources[1:]
        ]
    else:
        source_specs = [anywhere]
    result = pl.pallas_call(
        functools.partial(partial_beams_body, ranks, beams, edges, tables, len(before)),
        grid=(1,),
        out_shape=outs + ([weights] if tables else []),
        in_specs=[
            pl.BlockSpec((2, channels, pulses, width), lambda i: (0, 0, 0, chunk)),
            pl.BlockSpec(table.shape, lambda i: (0, 0)),
        ]
        + source_specs
        + [anywhere] * len(before),
        out_specs=[whole] * len(outs) + ([anywhere] if tables else []),
        scratch_shapes=[
            pltpu.VMEM((2, 2, width // LANES, pulses, LANES), F32),
            pltpu.VMEM((2, ranks, 2 * pulses // ranks, width), BF16),
            pltpu.VMEM((groups, channels * ranks, 16, width), BF16),
            pltpu.VMEM(weights.shape, BF16),
            pltpu.SemaphoreType.DMA,
            pltpu.VMEM((ranks * groups * 8 + TILE, 2 * beams * channels), F32),
            pltpu.VMEM((2, rows, beams * channels * ranks * 2), F32),
        ],
        compiler_params=pltpu.CompilerParams(vmem_limit_bytes=VMEM_LIMIT),
        cost_estimate=SMALL_COST,
        name="partial_beams",
    )(echoes, table, *sources, *before)
    count = len(whole_slots)
    flag = count + 1 + len(edges)
    return result[:count], result[count], result[count + 1 : flag], result[flag], result[flag + 1 :]


def summed_body(terms, edges, *refs):
    ins, outs = refs[:terms], refs[-1 - len(edges) :]
    total = ins[0][...].astype(F32)
    for term in ins[1:]:
        total += term[...].astype(F32)
    total = total.astype(BF16)
    outs[0][...] = total
    for edge, edge_ref in zip(edges, outs[1:]):
        edge_ref[0, 0] = total[0, edge]


def summed_block(terms, edges, before=()):
    beams, tiles, rows, lanes = terms[0].shape
    block = pl.BlockSpec((1, tiles, rows, lanes), lambda i: (i, 0, 0, 0))
    single = pl.BlockSpec((1, 1, rows, lanes), lambda i: (i, 0, 0, 0))
    return pl.pallas_call(
        functools.partial(summed_body, len(terms), edges),
        grid=(beams,),
        out_shape=[jax.ShapeDtypeStruct(terms[0].shape, BF16)]
        + [jax.ShapeDtypeStruct((beams, 1, rows, lanes), BF16)] * len(edges),
        in_specs=[block] * len(terms) + [pl.BlockSpec(memory_space=pl.ANY)] * len(before),
        out_specs=[block] + [single] * len(edges),
        compiler_params=pltpu.CompilerParams(vmem_limit_bytes=VMEM_LIMIT),
        cost_estimate=SMALL_COST,
        name="summed_block",
    )(*terms, *before)


def toeplitz_body(replica_ref, out_ref):
    chirp = replica_ref.shape[1]
    span = chirp + LANES
    padded = jnp.concatenate(
        [replica_ref[...].astype(F32), jnp.zeros((2, LANES), F32)], axis=1
    )
    taps = []
    for part in range(2):
        rows = jnp.broadcast_to(padded[part : part + 1], (LANES, span))
        taps.append(pltpu.roll(rows, 0, 1, stride=1, stride_axis=0).T)
    real, imag = (tap.astype(BF16) for tap in taps)
    split = LANES // 2
    low, high = slice(0, split), slice(split, LANES)
    for part, (own, other) in enumerate(((real, -imag), (imag, real))):
        columns = jnp.concatenate(
            [own[:, low], other[:, low], other[:, high], own[:, high]], axis=1
        )
        for tile in range(span // LANES):
            first = (2 * tile + part) * LANES
            out_ref[first : first + LANES, :] = columns[tile * LANES : (tile + 1) * LANES]


def toeplitz_taps(replica):
    return pl.pallas_call(
        toeplitz_body,
        out_shape=jax.ShapeDtypeStruct((2 * (replica.shape[1] + LANES), 2 * LANES), BF16),
        cost_estimate=SMALL_COST,
        name="toeplitz_taps",
    )(replica)


def tiles_body(tracks, count, place_ref, flag_ref, taps_ref, repeat_ref, gather_ref, *rest):
    pieces, (out_ref, line_ref, cut_ref) = rest[:count], rest[-3:]
    entry = pl.program_id(0)
    rows = pieces[0].shape[2]
    span = taps_ref.shape[0] // (2 * LANES)
    columns = [(piece, tile) for piece in pieces for tile in range(piece.shape[1])]
    for block in range(len(columns) - span + 1):
        window = [piece[0, tile] for piece, tile in columns[block : block + span]]
        product = jnp.dot(
            jnp.concatenate(window, axis=1), taps_ref[...], preferred_element_type=F32
        )
        if block == 0:
            product = jnp.where(flag_ref[:1, :1] == 0.0, 0.0, product)
        line_ref[2 * block * rows : (2 * block + 1) * rows, :] = product[:, :LANES]
        line_ref[(2 * block + 1) * rows : (2 * block + 2) * rows, :] = product[:, LANES:]

    lane_id = lax.broadcasted_iota(jnp.int32, (TILE, LANES), 1) % (LANES // 2)
    batch = 16

    def cut(step, carry):
        values = []
        for within in range(batch):
            track = step * batch + within
            row = place_ref[0, entry, track]
            low = line_ref[pl.ds(row, TILE), :]
            high = line_ref[pl.ds(row + rows, TILE), :]
            values.append(jnp.where(lane_id >= place_ref[1, entry, track], low, high))
        values = [
            pltpu.roll(value, place_ref[2, entry, step * batch + within], 1)
            for within, value in enumerate(values)
        ]
        here = pl.ds(pl.multiple_of(step * batch * TILE, batch * TILE), batch * TILE)
        cut_ref[here, :] = jnp.concatenate(values, axis=0).astype(BF16)
        return carry

    lax.fori_loop(0, tracks // batch, cut, 0)

    group = 2 * LANES
    many = divisor_up_to(tracks * TILE // group, 4) * group
    row_id = lax.broadcasted_iota(jnp.int32, (many, group), 0) % 8
    wanted = row_id == lax.broadcasted_iota(jnp.int32, (many, group), 1) % LANES // TILE
    for start in range(0, tracks * TILE, many):
        repeated = jnp.dot(
            cut_ref[start : start + many, :], repeat_ref[...], preferred_element_type=F32
        )
        masked = jnp.where(wanted, repeated, 0.0).astype(BF16)
        for first in range(0, many, group):
            value = jnp.dot(
                gather_ref[...], masked[first : first + group], preferred_element_type=F32
            )
            here = (start + first) // 8
            out_ref[0, here : here + group // 8, :] = value.astype(BF16)


def slots_body(terms, slot_ref, *rest):
    parts, (out_ref, total_ref, sorted_ref) = rest[:terms], rest[-3:]
    total = parts[0][0].astype(F32)
    for part in parts[1:]:
        total += part[0].astype(F32)
    for part in range(2):
        total_ref[part] = total[:, part * LANES : (part + 1) * LANES]
    sorted_ref[...] = jnp.zeros(sorted_ref.shape, F32)

    def move(track, carry):
        target = pl.ds(slot_ref[track] * 2, 2)
        sorted_ref[:, target, :] = total_ref[:, pl.ds(track * 2, 2), :]
        return carry

    lax.fori_loop(0, slot_ref.shape[0], move, 0, unroll=8)
    for part in range(2):
        out_ref[:, part * LANES : (part + 1) * LANES] = sorted_ref[part].astype(BF16)


def slotted(terms, slots, slot_total):
    count, lanes = terms[0][0].shape[1:]
    return pl.pallas_call(
        functools.partial(slots_body, len(terms)),
        grid=(1,),
        out_shape=jax.ShapeDtypeStruct((slot_total * 2, lanes), BF16),
        in_specs=[pl.BlockSpec(memory_space=pltpu.SMEM)]
        + [
            pl.BlockSpec((1, count, lanes), lambda i, entry=entry: (entry, 0, 0))
            for _, entry in terms
        ],
        out_specs=pl.BlockSpec((slot_total * 2, lanes), lambda i: (0, 0)),
        scratch_shapes=[
            pltpu.VMEM((2, count, LANES), F32),
            pltpu.VMEM((2, slot_total * 2, LANES), F32),
        ],
        compiler_params=pltpu.CompilerParams(vmem_limit_bytes=VMEM_LIMIT),
        cost_estimate=SMALL_COST,
        name="slotted_tiles",
    )(slots, *[term for term, _ in terms])


def cut_places(bins, gates, rows):
    first = gates + (LANES - HALF)
    half = LANES // 2
    return jnp.stack([first // half * rows + bins, first % half, (LANES - first % LANES) % LANES])


def beam_tiles(taps, pieces, places, flag, gate_len):
    _, entries, tracks = places.shape
    rows = pieces[0][0].shape[2]
    scalar = pl.BlockSpec(memory_space=pltpu.SMEM)
    blocks = gate_len // LANES + 2
    group = 2 * LANES
    column = np.arange(group)[None, :]
    repeat = np.arange(LANES)[:, None] == column // LANES * (LANES // 2) + column % TILE
    repeat = repeat.astype(ml_dtypes.bfloat16)
    gather = np.arange(group // 8)[:, None] == np.arange(group)[None, :] // 8
    gather = gather.astype(ml_dtypes.bfloat16)
    return pl.pallas_call(
        functools.partial(tiles_body, tracks, len(pieces)),
        grid=(entries,),
        out_shape=jax.ShapeDtypeStruct((entries, tracks * 2, group), BF16),
        in_specs=[
            scalar,
            pl.BlockSpec(flag.shape, lambda i: (0, 0)),
            pl.BlockSpec(taps.shape, lambda i: (0, 0)),
            pl.BlockSpec(repeat.shape, lambda i: (0, 0)),
            pl.BlockSpec(gather.shape, lambda i: (0, 0)),
        ]
        + [
            pl.BlockSpec((1,) + piece.shape[1:], lambda i, offset=offset: (i + offset, 0, 0, 0))
            for piece, offset in pieces
        ],
        out_specs=pl.BlockSpec((1, tracks * 2, group), lambda i: (i, 0, 0)),
        scratch_shapes=[
            pltpu.VMEM((2 * blocks * rows, LANES), F32),
            pltpu.VMEM((tracks * TILE, LANES), BF16),
        ],
        compiler_params=pltpu.CompilerParams(vmem_limit_bytes=VMEM_LIMIT),
        cost_estimate=SMALL_COST,
        name="beam_tiles",
    )(places, flag, taps, repeat, gather, *[piece for piece, _ in pieces])


def finish_body(*refs):
    parts, out_ref, wide_ref = refs[:-2], refs[-2], refs[-1]
    rows = out_ref.shape[0]
    for beam, part in enumerate(parts):
        for side in range(2):
            wide_ref[...] = part[:, side * LANES : (side + 1) * LANES].astype(F32)
            for half in range(2):
                column = ((side * len(parts) + beam) * 2 + half) * LANES
                out_ref[:, column : column + LANES] = wide_ref[pl.ds(half, rows, stride=2), :]


def finished(parts, rows):
    whole = pl.BlockSpec(memory_space=pltpu.VMEM)
    return pl.pallas_call(
        finish_body,
        out_shape=jax.ShapeDtypeStruct((rows, len(parts) * 4 * LANES), F32),
        in_specs=[whole] * len(parts),
        out_specs=whole,
        scratch_shapes=[pltpu.VMEM((rows * 2, LANES), F32)],
        compiler_params=pltpu.CompilerParams(vmem_limit_bytes=32 * 2**20),
        cost_estimate=SMALL_COST,
        name="finished_tiles",
    )(*parts)


def local(echoes, replica, beam_weights, track_doppler, track_gate, track_owner):
    gate_len = echoes.shape[3]
    chirp = replica.shape[1]
    _, beams, _, bins = beam_weights.shape
    ranks = lax.axis_size("pulse")
    owners = ranks * lax.axis_size("gate")
    table = pulse_table(bins, echoes.shape[2] // ranks)

    track_count = track_owner.shape[0]
    capacity = max(2, 5 * track_count // (2 * owners))
    owner_match = (
        track_owner[:, None] == jnp.arange(owners, dtype=jnp.int32)[None, :]
    ).astype(jnp.int32)
    running = jnp.cumsum(owner_match, axis=0, dtype=jnp.int32)
    slot_rank = jnp.sum(running * owner_match, axis=1, dtype=jnp.int32) - 1
    slots = track_owner * capacity + slot_rank
    place = jnp.stack([track_doppler % bins, track_gate % gate_len])

    def exchanged(value, slot):
        return lax.ppermute(value, "pulse", [(rank, rank ^ slot) for rank in range(ranks)])

    whole_slots, cut_slots = slot_kinds(ranks)

    width = gate_len // 2
    last_tile = width // LANES - 1
    spare_chunk, spare_steps = chirp % gate_len // width, chirp // gate_len + 1
    halo_chunks = [(position // gate_len + 1, position % gate_len // width) for position in range(0, chirp, width)]
    edges = [[], [last_tile]]
    edges[spare_chunk] = [0] + edges[spare_chunk]

    rows = bins + TILE
    place = cut_places(place[0], place[1], rows)
    far_places = [exchanged(place, slot) for slot in cut_slots]
    place = place[:, None]
    sources = weight_tables(beam_weights, chirp)
    far_places = jnp.stack(
        [item for item in far_places for _ in range(beams)], axis=1
    )
    taps = toeplitz_taps(replica)
    first_blocks, far, far_edges, flag, weights = partial_beams(
        echoes, table, sources, beams, 0, width, edges[0], before=[taps, far_places]
    )
    fars, ends = [far], [far_edges]
    flag = passed_along(flag, "gate", 1)
    second_blocks, far, far_edges, _, _ = partial_beams(
        echoes, table, weights, beams, 1, width, edges[1], before=[flag]
    )
    fars, ends = fars + [far], ends + [far_edges]

    def with_halo(full, spare, left):
        before = passed_along(left, "gate", 1)
        after = [passed_along(full[chunk], "gate", -steps) for steps, chunk in halo_chunks]
        return [before] + full + after + [passed_along(spare, "gate", -spare_steps)]

    def neighbours(blocks):
        return [blocks[0]] + [
            exchanged(blocks[kind], whole_slots[kind]) for kind in range(1, len(whole_slots))
        ]

    first = summed_block(neighbours(first_blocks), edges[0])
    far_pieces = with_halo(fars, ends[spare_chunk][0], ends[1][-1])
    far_tiles = beam_tiles(taps, [(piece, 0) for piece in far_pieces], far_places, flag, gate_len)
    second = summed_block(neighbours(second_blocks), edges[1], before=[far_tiles])
    arrived = [
        exchanged(far_tiles[kind * beams : (kind + 1) * beams], slot)
        for kind, slot in enumerate(cut_slots)
    ]
    own_pieces = with_halo([first[0], second[0]], [first, second][spare_chunk][1], second[-1])
    results = []
    for beam in range(beams):
        tiles = beam_tiles(
            taps, [(piece, beam) for piece in own_pieces], place, flag, gate_len
        )
        tiles = slotted(
            [(tiles, 0)] + [(item, beam) for item in arrived], slots, owners * capacity
        )
        sent = lax.all_to_all(
            tiles.reshape(owners, capacity * 2, 2 * LANES),
            ("pulse", "gate"),
            split_axis=0,
            concat_axis=0,
            tiled=True,
        )
        results.append(sent.reshape(owners * capacity * 2, 2 * LANES))
    return finished(results, owners * capacity)


def solution(mesh):
    return jax.shard_map(
        local,
        mesh=mesh,
        in_specs=(
            P(None, None, "pulse", "gate"),
            P(),
            P(None, None, None, "pulse"),
            P(("pulse", "gate")),
            P(("pulse", "gate")),
            P(("pulse", "gate")),
        ),
        out_specs=P(("pulse", "gate"), None),
        check_vma=False,
    )
```

```python
import functools
import math

import jax
import jax.numpy as jnp
import ml_dtypes
import numpy as np
from jax import lax
from jax.experimental import pallas as pl
from jax.experimental.pallas import tpu as pltpu
from jax.sharding import PartitionSpec as P

TILE = 16
HALF = TILE // 2
LANES = 128
F32 = jnp.float32
BF16 = jnp.bfloat16
VMEM_LIMIT = 63 * 2**20
SMALL_COST = pl.CostEstimate(flops=2**20, bytes_accessed=2**16, transcendentals=0)


def passed_along(value, axis, steps):
    count = lax.axis_size(axis)
    leading, last = (max(0, -steps), min(count, count - steps))
    return lax.ppermute(value, axis, [(source, source + steps) for source in range(leading, last)])


def pulse_table(bins, depth):
    angle = 2.0 * np.pi * (np.outer(np.arange(bins), np.arange(depth)) % bins) / bins
    cos_part, sin_part = np.cos(angle), np.sin(angle)
    table = np.stack(
        [np.concatenate([cos_part, sin_part], 1), np.concatenate([-sin_part, cos_part], 1)]
    )
    table = table.reshape(2, bins // 8, 8, 2 * depth).transpose(1, 0, 2, 3)
    return table.reshape(2 * bins, 2 * depth).astype(ml_dtypes.bfloat16)


def gather_lines(me, parts, line_ref):
    count, bins = line_ref.shape[1], parts[0].shape[1]
    ends = jnp.zeros((HALF, count), F32)
    line_ref[:HALF, :] = ends
    line_ref[HALF + len(parts) * bins :, :] = ends
    for slot, part in enumerate(parts):
        first = pl.multiple_of((slot ^ me) * bins + HALF, 8)
        line_ref[pl.ds(first, bins), :] = part[:count, :].T


def quarter_turns(turn, ranks):
    cos_part = jnp.ones(turn.shape, F32)
    sin_part = jnp.zeros(turn.shape, F32)
    for value in range(1, ranks):
        angle = 2 * math.pi * value / ranks
        cos_part = jnp.where(turn == value, round(math.cos(angle), 12), cos_part)
        sin_part = jnp.where(turn == value, round(math.sin(angle), 12), sin_part)
    return cos_part, sin_part


def turn_tables(ranks, me, cos_ref, sin_ref, turned_ref):
    rows, lanes = cos_ref.shape
    offset = lax.broadcasted_iota(jnp.int32, (rows, lanes), 0) + (ranks * 8 - HALF)
    turn_cos, turn_sin = quarter_turns((me * offset) & (ranks - 1), ranks)
    base_cos, base_sin = cos_ref[...], sin_ref[...]
    turned_ref[0] = turn_cos * base_cos - turn_sin * base_sin
    turned_ref[1] = turn_sin * base_cos + turn_cos * base_sin


def fill_weights(ranks, bins, slot, me, line_ref, turned_ref, select_ref, weight_ref):
    groups, pairs, _, depth = weight_ref.shape
    per = divisor_up_to(groups, 11)
    span = per * 8
    lanes = turned_ref.shape[2]
    lane_id = lax.broadcasted_iota(jnp.int32, (8, lanes), 1)
    block = slot ^ me
    slot_cos, slot_sin = quarter_turns((block * (lane_id // 2 % ranks)) & (ranks - 1), ranks)
    first_part = lane_id[:1] % 2 == 0
    slot_cos, slot_sin = slot_cos[:1], slot_sin[:1]
    own_cos = jnp.where(first_part, slot_cos, slot_sin)
    own_sin = jnp.where(first_part, -slot_sin, slot_cos)
    cells = (span * 2, LANES)
    column = lax.broadcasted_iota(jnp.int32, cells, 1)
    diagonal = lax.broadcasted_iota(jnp.int32, cells, 0) % 8 == column % 8
    source_lane = column // 8
    for step in range(groups // per):
        here = slice(step * span, (step + 1) * span)
        rows = line_ref[pl.ds(pl.multiple_of(block * bins + step * span, 8), span), :]
        high = rows.astype(BF16)
        low = (rows - high.astype(F32)).astype(BF16)
        wide = jnp.dot(high, select_ref[...], preferred_element_type=F32) + jnp.dot(
            low, select_ref[...], preferred_element_type=F32
        )
        base_cos, base_sin = turned_ref[0, here, :], turned_ref[1, here, :]
        own = base_cos * own_cos + base_sin * own_sin
        other = base_sin * own_cos - base_cos * own_sin
        real, imag = wide[:, :lanes], wide[:, lanes:]
        out_real = (real * own + imag * other).reshape(per, 8, lanes)
        out_imag = (imag * own - real * other).reshape(per, 8, lanes)
        both = jnp.concatenate([out_real, out_imag], axis=1).reshape(span * 2, lanes)
        for first in range(0, lanes * 8, LANES):
            source = first // 8 // LANES * LANES
            wide = jnp.take_along_axis(
                both[:, source : source + LANES],
                source_lane + (first // 8 - source),
                axis=1,
                mode="promise_in_bounds",
            )
            wide = jnp.where(diagonal, wide, 0.0).astype(BF16).reshape(per, 16, LANES)
            lane = first % depth
            weight_ref[
                step * per : (step + 1) * per,
                first // depth * ranks + slot,
                :,
                lane : lane + LANES,
            ] = wide


def divisor_up_to(value, limit):
    return max(step for step in range(1, limit + 1) if value % step == 0)


def weight_tables(beam_weights, pulse_len):
    _, beams, channels, bins = beam_weights.shape
    ranks = lax.axis_size("pulse")
    total = bins * ranks
    count = 2 * beams * channels
    flat = beam_weights.reshape(count, bins)
    parts = [flat] + [
        lax.ppermute(flat, "pulse", [(rank, rank ^ slot) for rank in range(ranks)])
        for slot in range(1, ranks)
    ]
    small = channels * ranks * 2
    phase = np.arange(small) // 2 % ranks
    angle = 2.0 * np.pi * (np.outer(np.arange(bins + TILE) - HALF, phase) % total) / total
    scale = 1.0 / math.sqrt(total * 2.0 * pulse_len)
    base_cos = np.tile(np.cos(angle) * scale, (1, beams)).astype(np.float32)
    base_sin = np.tile(np.sin(angle) * scale, (1, beams)).astype(np.float32)
    target = np.arange(2 * beams * small)[None, :]
    wanted = target // small * channels + target % small // (2 * ranks)
    select = (np.arange(count)[:, None] == wanted).astype(ml_dtypes.bfloat16)
    me = lax.axis_index("pulse").reshape(1)
    return [me] + parts + [base_cos, base_sin, select]


def slot_kinds(ranks):
    whole_slots = [slot for slot in range(ranks) if slot & (slot - 1) == 0]
    return whole_slots, [slot for slot in range(ranks) if slot not in whole_slots]


def partial_beams_body(ranks, beams, edges, tables, before, echo_ref, table_ref, *rest):
    sources, rest = rest[: max(tables, 1)], rest[max(tables, 1) + before :]
    outs, (wide_ref, taken_ref, stage_ref, weight_ref, weight_sem) = rest[:-7], rest[-7:-2]
    line_ref, turned_ref = rest[-2:]
    whole_slots, cut_slots = slot_kinds(ranks)
    count = len(whole_slots)
    far_ref, edge_refs, flag_ref = outs[count], outs[count + 1 : count + 1 + len(edges)], outs[count + 1 + len(edges)]
    flag_ref[...] = jnp.ones(flag_ref.shape, F32)
    _, channels, pulses, width = echo_ref.shape
    depth = pulses // ranks
    groups = table_ref.shape[0] // 16
    columns = width // LANES
    turns = channels // 2
    if tables:
        me = sources[0][0]
        bins = sources[1].shape[1]
        gather_lines(me, sources[1 : 1 + ranks], line_ref)
        turn_tables(ranks, me, *sources[1 + ranks : 3 + ranks], turned_ref)

        def weights_of(slot):
            fill_weights(ranks, bins, slot, me, line_ref, turned_ref, sources[-1], weight_ref)

        if ranks % turns:
            lax.fori_loop(0, ranks, lambda slot, carry: (weights_of(slot), carry)[1], 0)
    else:
        fetch = pltpu.make_async_copy(sources[0], weight_ref, weight_sem)
        fetch.start()

    def deinterleave(channel, side):
        for part in range(2):
            wide = echo_ref[part, channel].astype(F32)
            for column in range(columns):
                wide_ref[side, part, column] = wide[:, column * LANES : (column + 1) * LANES]
        for phase in range(ranks):
            here = pl.ds(phase, depth, stride=ranks)
            for part in range(2):
                for column in range(columns):
                    taken_ref[
                        side,
                        phase,
                        part * depth : (part + 1) * depth,
                        column * LANES : (column + 1) * LANES,
                    ] = wide_ref[side, part, column, here, :].astype(BF16)

    def transform(channel, side):
        for phase in range(ranks):
            product = jnp.dot(
                table_ref[...], taken_ref[side, phase], preferred_element_type=F32
            )
            stage_ref[:, channel * ranks + phase] = product.astype(BF16).reshape(groups, 16, width)

    deinterleave(0, 0)

    def two_channels(step, carry):
        first = step * 2
        deinterleave(first + 1, 1)
        transform(first, 0)
        deinterleave(lax.min(first + 2, channels - 1), 0)
        transform(first + 1, 1)
        if tables and ranks % turns == 0:
            for within in range(ranks // turns):
                weights_of(step * (ranks // turns) + within)
        return carry

    lax.fori_loop(0, turns, two_channels, 0)
    if tables:
        keep = pltpu.make_async_copy(weight_ref, outs[-1], weight_sem)
        keep.start()
    else:
        fetch.wait()

    _, pairs, _, inner = weight_ref.shape
    lines = pairs * 2
    steps = weight_ref.shape[0] // 2
    per = divisor_up_to(steps, 4)

    def combine(turn, carry):
        for within in range(per):
            step = turn * per + within
            halves = []
            for half in range(2):
                group = step * 2 + half
                source = lax.rem(group + groups - 1, groups)
                data = stage_ref[source].reshape(inner, width)
                weight = weight_ref[group].reshape(lines * 8, inner)
                product = jnp.dot(weight, data, preferred_element_type=F32)
                halves.append(product.reshape(lines, 8, width))
            both = jnp.concatenate(halves, axis=1).astype(BF16)
            here = pl.ds(pl.multiple_of(step * 16, 16), 16)
            for line in range(lines):
                beam, slot, part = line // (2 * ranks), line // 2 % ranks, line % 2
                value = both[line]
                for tile in range(columns):
                    piece = value[:, tile * LANES : (tile + 1) * LANES]
                    lanes = slice(part * LANES, (part + 1) * LANES)
                    if slot in whole_slots:
                        outs[whole_slots.index(slot)][beam, tile, here, lanes] = piece
                        continue
                    entry = cut_slots.index(slot) * beams + beam
                    far_ref[entry, tile, here, lanes] = piece
                    for edge, edge_ref in zip(edges, edge_refs):
                        if edge == tile:
                            edge_ref[entry, 0, here, lanes] = piece
        return carry

    lax.fori_loop(0, steps // per, combine, 0)
    if tables:
        keep.wait()


def partial_beams(echoes, table, sources, beams, chunk, width, edges, before=()):
    _, channels, pulses, _ = echoes.shape
    ranks = lax.axis_size("pulse")
    groups = table.shape[0] // 16
    rows = groups * 8 + TILE
    whole_slots, cut_slots = slot_kinds(ranks)
    far = len(cut_slots) * beams
    tiles = width // LANES
    tables = len(sources) if len(sources) > 1 else 0
    weights = jax.ShapeDtypeStruct((rows // 8, beams * ranks, 16, channels * ranks * 16), BF16)
    outs = [jax.ShapeDtypeStruct((beams, tiles, rows, 2 * LANES), BF16)] * len(whole_slots)
    outs += [jax.ShapeDtypeStruct((far, tiles, rows, 2 * LANES), BF16)]
    outs += [jax.ShapeDtypeStruct((far, 1, rows, 2 * LANES), BF16)] * len(edges)
    outs += [jax.ShapeDtypeStruct((8, LANES), F32)]
    whole = pl.BlockSpec(memory_space=pltpu.VMEM)
    anywhere = pl.BlockSpec(memory_space=pl.ANY)
    if tables:
        source_specs = [pl.BlockSpec(memory_space=pltpu.SMEM)] + [
            pl.BlockSpec(item.shape, lambda i: (0, 0)) for item in sources[1:]
        ]
    else:
        source_specs = [anywhere]
    result = pl.pallas_call(
        functools.partial(partial_beams_body, ranks, beams, edges, tables, len(before)),
        grid=(1,),
        out_shape=outs + ([weights] if tables else []),
        in_specs=[
            pl.BlockSpec((2, channels, pulses, width), lambda i: (0, 0, 0, chunk)),
            pl.BlockSpec(table.shape, lambda i: (0, 0)),
        ]
        + source_specs
        + [anywhere] * len(before),
        out_specs=[whole] * len(outs) + ([anywhere] if tables else []),
        scratch_shapes=[
            pltpu.VMEM((2, 2, width // LANES, pulses, LANES), F32),
            pltpu.VMEM((2, ranks, 2 * pulses // ranks, width), BF16),
            pltpu.VMEM((groups, channels * ranks, 16, width), BF16),
            pltpu.VMEM(weights.shape, BF16),
            pltpu.SemaphoreType.DMA,
            pltpu.VMEM((ranks * groups * 8 + TILE, 2 * beams * channels), F32),
            pltpu.VMEM((2, rows, beams * channels * ranks * 2), F32),
        ],
        compiler_params=pltpu.CompilerParams(vmem_limit_bytes=VMEM_LIMIT),
        cost_estimate=SMALL_COST,
        name="partial_beams",
    )(echoes, table, *sources, *before)
    count = len(whole_slots)
    flag = count + 1 + len(edges)
    return result[:count], result[count], result[count + 1 : flag], result[flag], result[flag + 1 :]


def summed_body(terms, edges, *refs):
    ins, outs = refs[:terms], refs[-1 - len(edges) :]
    total = ins[0][...].astype(F32)
    for term in ins[1:]:
        total += term[...].astype(F32)
    total = total.astype(BF16)
    outs[0][...] = total
    for edge, edge_ref in zip(edges, outs[1:]):
        edge_ref[0, 0] = total[0, edge]


def summed_block(terms, edges, before=()):
    beams, tiles, rows, lanes = terms[0].shape
    block = pl.BlockSpec((1, tiles, rows, lanes), lambda i: (i, 0, 0, 0))
    single = pl.BlockSpec((1, 1, rows, lanes), lambda i: (i, 0, 0, 0))
    return pl.pallas_call(
        functools.partial(summed_body, len(terms), edges),
        grid=(beams,),
        out_shape=[jax.ShapeDtypeStruct(terms[0].shape, BF16)]
        + [jax.ShapeDtypeStruct((beams, 1, rows, lanes), BF16)] * len(edges),
        in_specs=[block] * len(terms) + [pl.BlockSpec(memory_space=pl.ANY)] * len(before),
        out_specs=[block] + [single] * len(edges),
        compiler_params=pltpu.CompilerParams(vmem_limit_bytes=VMEM_LIMIT),
        cost_estimate=SMALL_COST,
        name="summed_block",
    )(*terms, *before)


def toeplitz_body(replica_ref, through_ref, out_ref, through_out):
    chirp = replica_ref.shape[1]
    span = chirp + LANES
    padded = jnp.concatenate(
        [replica_ref[...].astype(F32), jnp.zeros((2, LANES), F32)], axis=1
    )
    taps = []
    for part in range(2):
        rows = jnp.broadcast_to(padded[part : part + 1], (LANES, span))
        taps.append(pltpu.roll(rows, 0, 1, stride=1, stride_axis=0).T)
    real, imag = (tap.astype(BF16) for tap in taps)
    split = LANES // 2
    low, high = slice(0, split), slice(split, LANES)
    for part, (own, other) in enumerate(((real, -imag), (imag, real))):
        columns = jnp.concatenate(
            [own[:, low], other[:, low], other[:, high], own[:, high]], axis=1
        )
        for tile in range(span // LANES):
            first = (2 * tile + part) * LANES
            out_ref[first : first + LANES, :] = columns[tile * LANES : (tile + 1) * LANES]


def toeplitz_taps(replica, through):
    anywhere = pl.BlockSpec(memory_space=pl.ANY)
    return pl.pallas_call(
        toeplitz_body,
        out_shape=[
            jax.ShapeDtypeStruct((2 * (replica.shape[1] + LANES), 2 * LANES), BF16),
            jax.ShapeDtypeStruct(through.shape, through.dtype),
        ],
        in_specs=[pl.BlockSpec(memory_space=pltpu.VMEM), anywhere],
        out_specs=[pl.BlockSpec(memory_space=pltpu.VMEM), anywhere],
        input_output_aliases={1: 1},
        cost_estimate=SMALL_COST,
        name="toeplitz_taps",
    )(replica, through)


def tiles_body(tracks, count, place_ref, flag_ref, taps_ref, repeat_ref, gather_ref, *rest):
    pieces, (out_ref, line_ref, cut_ref) = rest[:count], rest[-3:]
    entry = pl.program_id(0)
    rows = pieces[0].shape[2]
    span = taps_ref.shape[0] // (2 * LANES)
    columns = [(piece, tile) for piece in pieces for tile in range(piece.shape[1])]
    for block in range(len(columns) - span + 1):
        window = [piece[0, tile] for piece, tile in columns[block : block + span]]
        product = jnp.dot(
            jnp.concatenate(window, axis=1), taps_ref[...], preferred_element_type=F32
        )
        if block == 0:
            product = jnp.where(flag_ref[:1, :1] == 0.0, 0.0, product)
        line_ref[2 * block * rows : (2 * block + 1) * rows, :] = product[:, :LANES]
        line_ref[(2 * block + 1) * rows : (2 * block + 2) * rows, :] = product[:, LANES:]

    lane_id = lax.broadcasted_iota(jnp.int32, (TILE, LANES), 1) % (LANES // 2)
    batch = 16

    def cut(step, carry):
        values = []
        for within in range(batch):
            track = step * batch + within
            row = place_ref[0, entry, track]
            low = line_ref[pl.ds(row, TILE), :]
            high = line_ref[pl.ds(row + rows, TILE), :]
            values.append(jnp.where(lane_id >= place_ref[1, entry, track], low, high))
        values = [
            pltpu.roll(value, place_ref[2, entry, step * batch + within], 1)
            for within, value in enumerate(values)
        ]
        here = pl.ds(pl.multiple_of(step * batch * TILE, batch * TILE), batch * TILE)
        cut_ref[here, :] = jnp.concatenate(values, axis=0).astype(BF16)
        return carry

    lax.fori_loop(0, tracks // batch, cut, 0)

    group = 2 * LANES
    many = divisor_up_to(tracks * TILE // group, 4) * group
    row_id = lax.broadcasted_iota(jnp.int32, (many, group), 0) % 8
    wanted = row_id == lax.broadcasted_iota(jnp.int32, (many, group), 1) % LANES // TILE
    for start in range(0, tracks * TILE, many):
        repeated = jnp.dot(
            cut_ref[start : start + many, :], repeat_ref[...], preferred_element_type=F32
        )
        masked = jnp.where(wanted, repeated, 0.0).astype(BF16)
        for first in range(0, many, group):
            value = jnp.dot(
                gather_ref[...], masked[first : first + group], preferred_element_type=F32
            )
            here = (start + first) // 8
            out_ref[0, here : here + group // 8, :] = value.astype(BF16)


def slots_body(terms, slot_ref, *rest):
    parts, (out_ref, total_ref, sorted_ref) = rest[:terms], rest[-3:]
    total = parts[0][0].astype(F32)
    for part in parts[1:]:
        total += part[0].astype(F32)
    for part in range(2):
        total_ref[part] = total[:, part * LANES : (part + 1) * LANES]
    sorted_ref[...] = jnp.zeros(sorted_ref.shape, F32)

    def move(track, carry):
        target = pl.ds(slot_ref[track] * 2, 2)
        sorted_ref[:, target, :] = total_ref[:, pl.ds(track * 2, 2), :]
        return carry

    lax.fori_loop(0, slot_ref.shape[0], move, 0, unroll=8)
    for part in range(2):
        out_ref[:, part * LANES : (part + 1) * LANES] = sorted_ref[part].astype(BF16)


def slotted(terms, slots, slot_total):
    count, lanes = terms[0][0].shape[1:]
    return pl.pallas_call(
        functools.partial(slots_body, len(terms)),
        grid=(1,),
        out_shape=jax.ShapeDtypeStruct((slot_total * 2, lanes), BF16),
        in_specs=[pl.BlockSpec(memory_space=pltpu.SMEM)]
        + [
            pl.BlockSpec((1, count, lanes), lambda i, entry=entry: (entry, 0, 0))
            for _, entry in terms
        ],
        out_specs=pl.BlockSpec((slot_total * 2, lanes), lambda i: (0, 0)),
        scratch_shapes=[
            pltpu.VMEM((2, count, LANES), F32),
            pltpu.VMEM((2, slot_total * 2, LANES), F32),
        ],
        compiler_params=pltpu.CompilerParams(vmem_limit_bytes=VMEM_LIMIT),
        cost_estimate=SMALL_COST,
        name="slotted_tiles",
    )(slots, *[term for term, _ in terms])


def cut_places(bins, gates, rows):
    first = gates + (LANES - HALF)
    half = LANES // 2
    return jnp.stack([first // half * rows + bins, first % half, (LANES - first % LANES) % LANES])


def beam_tiles(taps, pieces, places, flag, gate_len):
    _, entries, tracks = places.shape
    rows = pieces[0][0].shape[2]
    scalar = pl.BlockSpec(memory_space=pltpu.SMEM)
    blocks = gate_len // LANES + 2
    group = 2 * LANES
    column = np.arange(group)[None, :]
    repeat = np.arange(LANES)[:, None] == column // LANES * (LANES // 2) + column % TILE
    repeat = repeat.astype(ml_dtypes.bfloat16)
    gather = np.arange(group // 8)[:, None] == np.arange(group)[None, :] // 8
    gather = gather.astype(ml_dtypes.bfloat16)
    return pl.pallas_call(
        functools.partial(tiles_body, tracks, len(pieces)),
        grid=(entries,),
        out_shape=jax.ShapeDtypeStruct((entries, tracks * 2, group), BF16),
        in_specs=[
            scalar,
            pl.BlockSpec(flag.shape, lambda i: (0, 0)),
            pl.BlockSpec(taps.shape, lambda i: (0, 0)),
            pl.BlockSpec(repeat.shape, lambda i: (0, 0)),
            pl.BlockSpec(gather.shape, lambda i: (0, 0)),
        ]
        + [
            pl.BlockSpec((1,) + piece.shape[1:], lambda i, offset=offset: (i + offset, 0, 0, 0))
            for piece, offset in pieces
        ],
        out_specs=pl.BlockSpec((1, tracks * 2, group), lambda i: (i, 0, 0)),
        scratch_shapes=[
            pltpu.VMEM((2 * blocks * rows, LANES), F32),
            pltpu.VMEM((tracks * TILE, LANES), BF16),
        ],
        compiler_params=pltpu.CompilerParams(vmem_limit_bytes=VMEM_LIMIT),
        cost_estimate=SMALL_COST,
        name="beam_tiles",
    )(places, flag, taps, repeat, gather, *[piece for piece, _ in pieces])


def finish_body(*refs):
    parts, out_ref, wide_ref = refs[:-2], refs[-2], refs[-1]
    rows = out_ref.shape[0]
    for beam, part in enumerate(parts):
        for side in range(2):
            wide_ref[...] = part[:, side * LANES : (side + 1) * LANES].astype(F32)
            for half in range(2):
                column = ((side * len(parts) + beam) * 2 + half) * LANES
                out_ref[:, column : column + LANES] = wide_ref[pl.ds(half, rows, stride=2), :]


def finished(parts, rows):
    whole = pl.BlockSpec(memory_space=pltpu.VMEM)
    return pl.pallas_call(
        finish_body,
        out_shape=jax.ShapeDtypeStruct((rows, len(parts) * 4 * LANES), F32),
        in_specs=[whole] * len(parts),
        out_specs=whole,
        scratch_shapes=[pltpu.VMEM((rows * 2, LANES), F32)],
        compiler_params=pltpu.CompilerParams(vmem_limit_bytes=32 * 2**20),
        cost_estimate=SMALL_COST,
        name="finished_tiles",
    )(*parts)


def local(echoes, replica, beam_weights, track_doppler, track_gate, track_owner):
    gate_len = echoes.shape[3]
    chirp = replica.shape[1]
    _, beams, _, bins = beam_weights.shape
    ranks = lax.axis_size("pulse")
    owners = ranks * lax.axis_size("gate")
    table = pulse_table(bins, echoes.shape[2] // ranks)

    track_count = track_owner.shape[0]
    capacity = max(2, 5 * track_count // (2 * owners))
    owner_match = (
        track_owner[:, None] == jnp.arange(owners, dtype=jnp.int32)[None, :]
    ).astype(jnp.int32)
    running = jnp.cumsum(owner_match, axis=0, dtype=jnp.int32)
    slot_rank = jnp.sum(running * owner_match, axis=1, dtype=jnp.int32) - 1
    slots = track_owner * capacity + slot_rank
    place = jnp.stack([track_doppler % bins, track_gate % gate_len])

    def exchanged(value, slot):
        return lax.ppermute(value, "pulse", [(rank, rank ^ slot) for rank in range(ranks)])

    whole_slots, cut_slots = slot_kinds(ranks)

    width = gate_len // 2
    last_tile = width // LANES - 1
    spare_chunk, spare_steps = chirp % gate_len // width, chirp // gate_len + 1
    halo_chunks = [(position // gate_len + 1, position % gate_len // width) for position in range(0, chirp, width)]
    edges = [[], [last_tile]]
    edges[spare_chunk] = [0] + edges[spare_chunk]

    rows = bins + TILE
    taps, place = toeplitz_taps(replica, cut_places(place[0], place[1], rows))
    far_places = [exchanged(place, slot) for slot in cut_slots]
    place = place[:, None]
    sources = weight_tables(beam_weights, chirp)
    far_places = jnp.stack(
        [item for item in far_places for _ in range(beams)], axis=1
    )
    first_blocks, far, far_edges, flag, weights = partial_beams(
        echoes, table, sources, beams, 0, width, edges[0], before=[taps]
    )
    fars, ends = [far], [far_edges]
    flag = passed_along(flag, "gate", 1)
    second_blocks, far, far_edges, _, _ = partial_beams(
        echoes, table, weights, beams, 1, width, edges[1], before=[flag]
    )
    fars, ends = fars + [far], ends + [far_edges]

    def with_halo(full, spare, left):
        before = passed_along(left, "gate", 1)
        after = [passed_along(full[chunk], "gate", -steps) for steps, chunk in halo_chunks]
        return [before] + full + after + [passed_along(spare, "gate", -spare_steps)]

    def neighbours(blocks):
        return [blocks[0]] + [
            exchanged(blocks[kind], whole_slots[kind]) for kind in range(1, len(whole_slots))
        ]

    first = summed_block(neighbours(first_blocks), edges[0])
    far_pieces = with_halo(fars, ends[spare_chunk][0], ends[1][-1])
    far_tiles = beam_tiles(taps, [(piece, 0) for piece in far_pieces], far_places, flag, gate_len)
    second = summed_block(neighbours(second_blocks), edges[1], before=[far_tiles])
    arrived = [
        exchanged(far_tiles[kind * beams : (kind + 1) * beams], slot)
        for kind, slot in enumerate(cut_slots)
    ]
    own_pieces = with_halo([first[0], second[0]], [first, second][spare_chunk][1], second[-1])
    results = []
    for beam in range(beams):
        tiles = beam_tiles(
            taps, [(piece, beam) for piece in own_pieces], place, flag, gate_len
        )
        tiles = slotted(
            [(tiles, 0)] + [(item, beam) for item in arrived], slots, owners * capacity
        )
        sent = lax.all_to_all(
            tiles.reshape(owners, capacity * 2, 2 * LANES),
            ("pulse", "gate"),
            split_axis=0,
            concat_axis=0,
            tiled=True,
        )
        results.append(sent.reshape(owners * capacity * 2, 2 * LANES))
    return finished(results, owners * capacity)


def solution(mesh):
    return jax.shard_map(
        local,
        mesh=mesh,
        in_specs=(
            P(None, None, "pulse", "gate"),
            P(),
            P(None, None, None, "pulse"),
            P(("pulse", "gate")),
            P(("pulse", "gate")),
            P(("pulse", "gate")),
        ),
        out_specs=P(("pulse", "gate"), None),
        check_vma=False,
    )
```

```python
import functools
import math

import jax
import jax.numpy as jnp
import ml_dtypes
import numpy as np
from jax import lax
from jax.experimental import pallas as pl
from jax.experimental.pallas import tpu as pltpu
from jax.sharding import PartitionSpec as P

TILE = 16
HALF = TILE // 2
LANES = 128
F32 = jnp.float32
BF16 = jnp.bfloat16
VMEM_LIMIT = 63 * 2**20
SMALL_COST = pl.CostEstimate(flops=2**20, bytes_accessed=2**16, transcendentals=0)


def passed_along(value, axis, steps):
    count = lax.axis_size(axis)
    leading, last = (max(0, -steps), min(count, count - steps))
    return lax.ppermute(value, axis, [(source, source + steps) for source in range(leading, last)])


def pulse_table(bins, depth):
    angle = 2.0 * np.pi * (np.outer(np.arange(bins), np.arange(depth)) % bins) / bins
    cos_part, sin_part = np.cos(angle), np.sin(angle)
    table = np.stack(
        [np.concatenate([cos_part, sin_part], 1), np.concatenate([-sin_part, cos_part], 1)]
    )
    table = table.reshape(2, bins // 8, 8, 2 * depth).transpose(1, 0, 2, 3)
    return table.reshape(2 * bins, 2 * depth).astype(ml_dtypes.bfloat16)


def gather_lines(me, parts, line_ref):
    count, bins = line_ref.shape[1], parts[0].shape[1]
    ends = jnp.zeros((HALF, count), F32)
    line_ref[:HALF, :] = ends
    line_ref[HALF + len(parts) * bins :, :] = ends
    for slot, part in enumerate(parts):
        first = pl.multiple_of((slot ^ me) * bins + HALF, 8)
        line_ref[pl.ds(first, bins), :] = part[:count, :].T


def quarter_turns(turn, ranks):
    cos_part = jnp.ones(turn.shape, F32)
    sin_part = jnp.zeros(turn.shape, F32)
    for value in range(1, ranks):
        angle = 2 * math.pi * value / ranks
        cos_part = jnp.where(turn == value, round(math.cos(angle), 12), cos_part)
        sin_part = jnp.where(turn == value, round(math.sin(angle), 12), sin_part)
    return cos_part, sin_part


def turn_tables(ranks, me, cos_ref, sin_ref, turned_ref):
    rows, lanes = cos_ref.shape
    offset = lax.broadcasted_iota(jnp.int32, (rows, lanes), 0) + (ranks * 8 - HALF)
    turn_cos, turn_sin = quarter_turns((me * offset) & (ranks - 1), ranks)
    base_cos, base_sin = cos_ref[...], sin_ref[...]
    turned_ref[0] = turn_cos * base_cos - turn_sin * base_sin
    turned_ref[1] = turn_sin * base_cos + turn_cos * base_sin


def fill_weights(ranks, bins, slot, me, line_ref, turned_ref, select_ref, weight_ref):
    groups, pairs, _, depth = weight_ref.shape
    per = divisor_up_to(groups, 11)
    span = per * 8
    lanes = turned_ref.shape[2]
    lane_id = lax.broadcasted_iota(jnp.int32, (8, lanes), 1)
    block = slot ^ me
    slot_cos, slot_sin = quarter_turns((block * (lane_id // 2 % ranks)) & (ranks - 1), ranks)
    first_part = lane_id[:1] % 2 == 0
    slot_cos, slot_sin = slot_cos[:1], slot_sin[:1]
    own_cos = jnp.where(first_part, slot_cos, slot_sin)
    own_sin = jnp.where(first_part, -slot_sin, slot_cos)
    cells = (span * 2, LANES)
    column = lax.broadcasted_iota(jnp.int32, cells, 1)
    diagonal = lax.broadcasted_iota(jnp.int32, cells, 0) % 8 == column % 8
    source_lane = column // 8
    for step in range(groups // per):
        here = slice(step * span, (step + 1) * span)
        rows = line_ref[pl.ds(pl.multiple_of(block * bins + step * span, 8), span), :]
        high = rows.astype(BF16)
        low = (rows - high.astype(F32)).astype(BF16)
        wide = jnp.dot(high, select_ref[...], preferred_element_type=F32) + jnp.dot(
            low, select_ref[...], preferred_element_type=F32
        )
        base_cos, base_sin = turned_ref[0, here, :], turned_ref[1, here, :]
        own = base_cos * own_cos + base_sin * own_sin
        other = base_sin * own_cos - base_cos * own_sin
        real, imag = wide[:, :lanes], wide[:, lanes:]
        out_real = (real * own + imag * other).reshape(per, 8, lanes)
        out_imag = (imag * own - real * other).reshape(per, 8, lanes)
        both = jnp.concatenate([out_real, out_imag], axis=1).reshape(span * 2, lanes)
        for first in range(0, lanes * 8, LANES):
            source = first // 8 // LANES * LANES
            wide = jnp.take_along_axis(
                both[:, source : source + LANES],
                source_lane + (first // 8 - source),
                axis=1,
                mode="promise_in_bounds",
            )
            wide = jnp.where(diagonal, wide, 0.0).astype(BF16).reshape(per, 16, LANES)
            lane = first % depth
            weight_ref[
                step * per : (step + 1) * per,
                first // depth * ranks + slot,
                :,
                lane : lane + LANES,
            ] = wide


def divisor_up_to(value, limit):
    return max(step for step in range(1, limit + 1) if value % step == 0)


def weight_tables(beam_weights, pulse_len):
    _, beams, channels, bins = beam_weights.shape
    ranks = lax.axis_size("pulse")
    total = bins * ranks
    count = 2 * beams * channels
    flat = beam_weights.reshape(count, bins)
    parts = [flat] + [
        lax.ppermute(flat, "pulse", [(rank, rank ^ slot) for rank in range(ranks)])
        for slot in range(1, ranks)
    ]
    small = channels * ranks * 2
    phase = np.arange(small) // 2 % ranks
    angle = 2.0 * np.pi * (np.outer(np.arange(bins + TILE) - HALF, phase) % total) / total
    scale = 1.0 / math.sqrt(total * 2.0 * pulse_len)
    base_cos = np.tile(np.cos(angle) * scale, (1, beams)).astype(np.float32)
    base_sin = np.tile(np.sin(angle) * scale, (1, beams)).astype(np.float32)
    target = np.arange(2 * beams * small)[None, :]
    wanted = target // small * channels + target % small // (2 * ranks)
    select = (np.arange(count)[:, None] == wanted).astype(ml_dtypes.bfloat16)
    me = lax.axis_index("pulse").reshape(1)
    return [me] + parts + [base_cos, base_sin, select]


def slot_kinds(ranks):
    whole_slots = [slot for slot in range(ranks) if slot & (slot - 1) == 0]
    return whole_slots, [slot for slot in range(ranks) if slot not in whole_slots]


def partial_beams_body(ranks, beams, edges, tables, before, echo_ref, table_ref, *rest):
    sources, rest = rest[: max(tables, 1)], rest[max(tables, 1) + before :]
    outs, (wide_ref, taken_ref, stage_ref, weight_ref, weight_sem) = rest[:-7], rest[-7:-2]
    line_ref, turned_ref = rest[-2:]
    whole_slots, cut_slots = slot_kinds(ranks)
    count = len(whole_slots)
    far_ref, edge_refs, flag_ref = outs[count], outs[count + 1 : count + 1 + len(edges)], outs[count + 1 + len(edges)]
    flag_ref[...] = jnp.ones(flag_ref.shape, F32)
    _, channels, pulses, width = echo_ref.shape
    depth = pulses // ranks
    groups = table_ref.shape[0] // 16
    columns = width // LANES
    turns = channels // 2
    if tables:
        me = sources[0][0]
        bins = sources[1].shape[1]
        gather_lines(me, sources[1 : 1 + ranks], line_ref)
        turn_tables(ranks, me, *sources[1 + ranks : 3 + ranks], turned_ref)

        def weights_of(slot):
            fill_weights(ranks, bins, slot, me, line_ref, turned_ref, sources[-1], weight_ref)

        if ranks % turns:
            lax.fori_loop(0, ranks, lambda slot, carry: (weights_of(slot), carry)[1], 0)
    else:
        fetch = pltpu.make_async_copy(sources[0], weight_ref, weight_sem)
        fetch.start()

    def deinterleave(channel, side):
        for part in range(2):
            wide = echo_ref[part, channel].astype(F32)
            for column in range(columns):
                wide_ref[side, part, column] = wide[:, column * LANES : (column + 1) * LANES]
        for phase in range(ranks):
            here = pl.ds(phase, depth, stride=ranks)
            for part in range(2):
                for column in range(columns):
                    taken_ref[
                        side,
                        phase,
                        part * depth : (part + 1) * depth,
                        column * LANES : (column + 1) * LANES,
                    ] = wide_ref[side, part, column, here, :].astype(BF16)

    def transform(channel, side):
        for phase in range(ranks):
            product = jnp.dot(
                table_ref[...], taken_ref[side, phase], preferred_element_type=F32
            )
            stage_ref[:, channel * ranks + phase] = product.astype(BF16).reshape(groups, 16, width)

    deinterleave(0, 0)

    def two_channels(step, carry):
        first = step * 2
        deinterleave(first + 1, 1)
        transform(first, 0)
        deinterleave(lax.min(first + 2, channels - 1), 0)
        transform(first + 1, 1)
        if tables and ranks % turns == 0:
            for within in range(ranks // turns):
                weights_of(step * (ranks // turns) + within)
        return carry

    lax.fori_loop(0, turns, two_channels, 0)
    if tables:
        keep = pltpu.make_async_copy(weight_ref, outs[-1], weight_sem)
        keep.start()
    else:
        fetch.wait()

    _, pairs, _, inner = weight_ref.shape
    lines = pairs * 2
    steps = weight_ref.shape[0] // 2
    per = divisor_up_to(steps, 4)

    def combine(turn, carry):
        for within in range(per):
            step = turn * per + within
            halves = []
            for half in range(2):
                group = step * 2 + half
                source = lax.rem(group + groups - 1, groups)
                data = stage_ref[source].reshape(inner, width)
                weight = weight_ref[group].reshape(lines * 8, inner)
                product = jnp.dot(weight, data, preferred_element_type=F32)
                halves.append(product.reshape(lines, 8, width))
            both = jnp.concatenate(halves, axis=1).astype(BF16)
            here = pl.ds(pl.multiple_of(step * 16, 16), 16)
            for line in range(lines):
                beam, slot, part = line // (2 * ranks), line // 2 % ranks, line % 2
                value = both[line]
                for tile in range(columns):
                    piece = value[:, tile * LANES : (tile + 1) * LANES]
                    lanes = slice(part * LANES, (part + 1) * LANES)
                    if slot in whole_slots:
                        outs[whole_slots.index(slot)][beam, tile, here, lanes] = piece
                        continue
                    entry = cut_slots.index(slot) * beams + beam
                    far_ref[entry, tile, here, lanes] = piece
                    for edge, edge_ref in zip(edges, edge_refs):
                        if edge == tile:
                            edge_ref[entry, 0, here, lanes] = piece
        return carry

    lax.fori_loop(0, steps // per, combine, 0)
    if tables:
        keep.wait()


def partial_beams(echoes, table, sources, beams, chunk, width, edges, before=()):
    _, channels, pulses, _ = echoes.shape
    ranks = lax.axis_size("pulse")
    groups = table.shape[0] // 16
    rows = groups * 8 + TILE
    whole_slots, cut_slots = slot_kinds(ranks)
    far = len(cut_slots) * beams
    tiles = width // LANES
    tables = len(sources) if len(sources) > 1 else 0
    weights = jax.ShapeDtypeStruct((rows // 8, beams * ranks, 16, channels * ranks * 16), BF16)
    outs = [jax.ShapeDtypeStruct((beams, tiles, rows, 2 * LANES), BF16)] * len(whole_slots)
    outs += [jax.ShapeDtypeStruct((far, tiles, rows, 2 * LANES), BF16)]
    outs += [jax.ShapeDtypeStruct((far, 1, rows, 2 * LANES), BF16)] * len(edges)
    outs += [jax.ShapeDtypeStruct((8, LANES), F32)]
    whole = pl.BlockSpec(memory_space=pltpu.VMEM)
    anywhere = pl.BlockSpec(memory_space=pl.ANY)
    if tables:
        source_specs = [pl.BlockSpec(memory_space=pltpu.SMEM)] + [
            pl.BlockSpec(item.shape, lambda i: (0, 0)) for item in sources[1:]
        ]
    else:
        source_specs = [anywhere]
    result = pl.pallas_call(
        functools.partial(partial_beams_body, ranks, beams, edges, tables, len(before)),
        grid=(1,),
        out_shape=outs + ([weights] if tables else []),
        in_specs=[
            pl.BlockSpec((2, channels, pulses, width), lambda i: (0, 0, 0, chunk)),
            pl.BlockSpec(table.shape, lambda i: (0, 0)),
        ]
        + source_specs
        + [anywhere] * len(before),
        out_specs=[whole] * len(outs) + ([anywhere] if tables else []),
        scratch_shapes=[
            pltpu.VMEM((2, 2, width // LANES, pulses, LANES), F32),
            pltpu.VMEM((2, ranks, 2 * pulses // ranks, width), BF16),
            pltpu.VMEM((groups, channels * ranks, 16, width), BF16),
            pltpu.VMEM(weights.shape, BF16),
            pltpu.SemaphoreType.DMA,
            pltpu.VMEM((ranks * groups * 8 + TILE, 2 * beams * channels), F32),
            pltpu.VMEM((2, rows, beams * channels * ranks * 2), F32),
        ],
        compiler_params=pltpu.CompilerParams(vmem_limit_bytes=VMEM_LIMIT),
        cost_estimate=SMALL_COST,
        name="partial_beams",
    )(echoes, table, *sources, *before)
    count = len(whole_slots)
    flag = count + 1 + len(edges)
    return result[:count], result[count], result[count + 1 : flag], result[flag], result[flag + 1 :]


def summed_body(terms, edges, *refs):
    ins, outs = refs[:terms], refs[-1 - len(edges) :]
    total = ins[0][...].astype(F32)
    for term in ins[1:]:
        total += term[...].astype(F32)
    total = total.astype(BF16)
    outs[0][...] = total
    for edge, edge_ref in zip(edges, outs[1:]):
        edge_ref[0, 0] = total[0, edge]


def summed_block(terms, edges, before=()):
    beams, tiles, rows, lanes = terms[0].shape
    block = pl.BlockSpec((1, tiles, rows, lanes), lambda i: (i, 0, 0, 0))
    single = pl.BlockSpec((1, 1, rows, lanes), lambda i: (i, 0, 0, 0))
    return pl.pallas_call(
        functools.partial(summed_body, len(terms), edges),
        grid=(beams,),
        out_shape=[jax.ShapeDtypeStruct(terms[0].shape, BF16)]
        + [jax.ShapeDtypeStruct((beams, 1, rows, lanes), BF16)] * len(edges),
        in_specs=[block] * len(terms) + [pl.BlockSpec(memory_space=pl.ANY)] * len(before),
        out_specs=[block] + [single] * len(edges),
        compiler_params=pltpu.CompilerParams(vmem_limit_bytes=VMEM_LIMIT),
        cost_estimate=SMALL_COST,
        name="summed_block",
    )(*terms, *before)


def toeplitz_body(replica_ref, out_ref):
    chirp = replica_ref.shape[1]
    span = chirp + LANES
    padded = jnp.concatenate(
        [replica_ref[...].astype(F32), jnp.zeros((2, LANES), F32)], axis=1
    )
    taps = []
    for part in range(2):
        rows = jnp.broadcast_to(padded[part : part + 1], (LANES, span))
        taps.append(pltpu.roll(rows, 0, 1, stride=1, stride_axis=0).T)
    real, imag = (tap.astype(BF16) for tap in taps)
    split = LANES // 2
    low, high = slice(0, split), slice(split, LANES)
    for part, (own, other) in enumerate(((real, -imag), (imag, real))):
        columns = jnp.concatenate(
            [own[:, low], other[:, low], other[:, high], own[:, high]], axis=1
        )
        for tile in range(span // LANES):
            first = (2 * tile + part) * LANES
            out_ref[first : first + LANES, :] = columns[tile * LANES : (tile + 1) * LANES]


def toeplitz_taps(replica):
    return pl.pallas_call(
        toeplitz_body,
        out_shape=jax.ShapeDtypeStruct((2 * (replica.shape[1] + LANES), 2 * LANES), BF16),
        cost_estimate=SMALL_COST,
        name="toeplitz_taps",
    )(replica)


def tiles_body(tracks, count, place_ref, flag_ref, taps_ref, repeat_ref, gather_ref, *rest):
    pieces, (out_ref, line_ref, cut_ref) = rest[:count], rest[-3:]
    entry = pl.program_id(0)
    rows = pieces[0].shape[2]
    span = taps_ref.shape[0] // (2 * LANES)
    columns = [(piece, tile) for piece in pieces for tile in range(piece.shape[1])]
    for block in range(len(columns) - span + 1):
        window = [piece[0, tile] for piece, tile in columns[block : block + span]]
        product = jnp.dot(
            jnp.concatenate(window, axis=1), taps_ref[...], preferred_element_type=F32
        )
        if block == 0:
            product = jnp.where(flag_ref[:1, :1] == 0.0, 0.0, product)
        line_ref[2 * block * rows : (2 * block + 1) * rows, :] = product[:, :LANES]
        line_ref[(2 * block + 1) * rows : (2 * block + 2) * rows, :] = product[:, LANES:]

    lane_id = lax.broadcasted_iota(jnp.int32, (TILE, LANES), 1) % (LANES // 2)
    batch = 16

    def cut(step, carry):
        values = []
        for within in range(batch):
            track = step * batch + within
            row = place_ref[0, entry, track]
            low = line_ref[pl.ds(row, TILE), :]
            high = line_ref[pl.ds(row + rows, TILE), :]
            values.append(jnp.where(lane_id >= place_ref[1, entry, track], low, high))
        values = [
            pltpu.roll(value, place_ref[2, entry, step * batch + within], 1)
            for within, value in enumerate(values)
        ]
        here = pl.ds(pl.multiple_of(step * batch * TILE, batch * TILE), batch * TILE)
        cut_ref[here, :] = jnp.concatenate(values, axis=0).astype(BF16)
        return carry

    lax.fori_loop(0, tracks // batch, cut, 0)

    group = 2 * LANES
    many = divisor_up_to(tracks * TILE // group, 4) * group
    row_id = lax.broadcasted_iota(jnp.int32, (many, group), 0) % 8
    wanted = row_id == lax.broadcasted_iota(jnp.int32, (many, group), 1) % LANES // TILE
    for start in range(0, tracks * TILE, many):
        repeated = jnp.dot(
            cut_ref[start : start + many, :], repeat_ref[...], preferred_element_type=F32
        )
        masked = jnp.where(wanted, repeated, 0.0).astype(BF16)
        for first in range(0, many, group):
            value = jnp.dot(
                gather_ref[...], masked[first : first + group], preferred_element_type=F32
            )
            here = (start + first) // 8
            out_ref[0, here : here + group // 8, :] = value.astype(BF16)


def slots_body(terms, slot_ref, *rest):
    parts, (out_ref, total_ref, sorted_ref) = rest[:terms], rest[-3:]
    total = parts[0][0].astype(F32)
    for part in parts[1:]:
        total += part[0].astype(F32)
    for part in range(2):
        here = pl.ds(part, total.shape[0], stride=2)
        total_ref[here, :] = total[:, part * LANES : (part + 1) * LANES]
    sorted_ref[...] = jnp.zeros(sorted_ref.shape, F32)

    def move(track, carry):
        sorted_ref[pl.ds(slot_ref[track] * 4, 4), :] = total_ref[pl.ds(track * 4, 4), :]
        return carry

    lax.fori_loop(0, slot_ref.shape[0], move, 0, unroll=8)
    out_ref[...] = sorted_ref[...].astype(BF16)


def slotted(terms, slots, slot_total):
    count, lanes = terms[0][0].shape[1:]
    return pl.pallas_call(
        functools.partial(slots_body, len(terms)),
        grid=(1,),
        out_shape=jax.ShapeDtypeStruct((slot_total * 4, LANES), BF16),
        in_specs=[pl.BlockSpec(memory_space=pltpu.SMEM)]
        + [
            pl.BlockSpec((1, count, lanes), lambda i, entry=entry: (entry, 0, 0))
            for _, entry in terms
        ],
        out_specs=pl.BlockSpec((slot_total * 4, LANES), lambda i: (0, 0)),
        scratch_shapes=[
            pltpu.VMEM((count * 2, LANES), F32),
            pltpu.VMEM((slot_total * 4, LANES), F32),
        ],
        compiler_params=pltpu.CompilerParams(vmem_limit_bytes=VMEM_LIMIT),
        cost_estimate=SMALL_COST,
        name="slotted_tiles",
    )(slots, *[term for term, _ in terms])


def cut_places(bins, gates, rows):
    first = gates + (LANES - HALF)
    half = LANES // 2
    return jnp.stack([first // half * rows + bins, first % half, (LANES - first % LANES) % LANES])


def beam_tiles(taps, pieces, places, flag, gate_len):
    _, entries, tracks = places.shape
    rows = pieces[0][0].shape[2]
    scalar = pl.BlockSpec(memory_space=pltpu.SMEM)
    blocks = gate_len // LANES + 2
    group = 2 * LANES
    column = np.arange(group)[None, :]
    repeat = np.arange(LANES)[:, None] == column // LANES * (LANES // 2) + column % TILE
    repeat = repeat.astype(ml_dtypes.bfloat16)
    gather = np.arange(group // 8)[:, None] == np.arange(group)[None, :] // 8
    gather = gather.astype(ml_dtypes.bfloat16)
    return pl.pallas_call(
        functools.partial(tiles_body, tracks, len(pieces)),
        grid=(entries,),
        out_shape=jax.ShapeDtypeStruct((entries, tracks * 2, group), BF16),
        in_specs=[
            scalar,
            pl.BlockSpec(flag.shape, lambda i: (0, 0)),
            pl.BlockSpec(taps.shape, lambda i: (0, 0)),
            pl.BlockSpec(repeat.shape, lambda i: (0, 0)),
            pl.BlockSpec(gather.shape, lambda i: (0, 0)),
        ]
        + [
            pl.BlockSpec((1,) + piece.shape[1:], lambda i, offset=offset: (i + offset, 0, 0, 0))
            for piece, offset in pieces
        ],
        out_specs=pl.BlockSpec((1, tracks * 2, group), lambda i: (i, 0, 0)),
        scratch_shapes=[
            pltpu.VMEM((2 * blocks * rows, LANES), F32),
            pltpu.VMEM((tracks * TILE, LANES), BF16),
        ],
        compiler_params=pltpu.CompilerParams(vmem_limit_bytes=VMEM_LIMIT),
        cost_estimate=SMALL_COST,
        name="beam_tiles",
    )(places, flag, taps, repeat, gather, *[piece for piece, _ in pieces])


def finish_body(*refs):
    parts, out_ref, wide_ref = refs[:-2], refs[-2], refs[-1]
    rows = out_ref.shape[0]
    for beam, part in enumerate(parts):
        wide_ref[...] = part[...].astype(F32)
        for half in range(2):
            for side in range(2):
                column = ((side * len(parts) + beam) * 2 + half) * LANES
                here = pl.ds(half * 2 + side, rows, stride=4)
                out_ref[:, column : column + LANES] = wide_ref[here, :]


def finished(parts, rows):
    whole = pl.BlockSpec(memory_space=pltpu.VMEM)
    return pl.pallas_call(
        finish_body,
        out_shape=jax.ShapeDtypeStruct((rows, len(parts) * 4 * LANES), F32),
        in_specs=[whole] * len(parts),
        out_specs=whole,
        scratch_shapes=[pltpu.VMEM((rows * 4, LANES), F32)],
        compiler_params=pltpu.CompilerParams(vmem_limit_bytes=32 * 2**20),
        cost_estimate=SMALL_COST,
        name="finished_tiles",
    )(*parts)


def local(echoes, replica, beam_weights, track_doppler, track_gate, track_owner):
    gate_len = echoes.shape[3]
    chirp = replica.shape[1]
    _, beams, _, bins = beam_weights.shape
    ranks = lax.axis_size("pulse")
    owners = ranks * lax.axis_size("gate")
    table = pulse_table(bins, echoes.shape[2] // ranks)

    track_count = track_owner.shape[0]
    capacity = max(2, 5 * track_count // (2 * owners))
    owner_match = (
        track_owner[:, None] == jnp.arange(owners, dtype=jnp.int32)[None, :]
    ).astype(jnp.int32)
    running = jnp.cumsum(owner_match, axis=0, dtype=jnp.int32)
    slot_rank = jnp.sum(running * owner_match, axis=1, dtype=jnp.int32) - 1
    slots = track_owner * capacity + slot_rank
    place = jnp.stack([track_doppler % bins, track_gate % gate_len])

    def exchanged(value, slot):
        return lax.ppermute(value, "pulse", [(rank, rank ^ slot) for rank in range(ranks)])

    whole_slots, cut_slots = slot_kinds(ranks)

    width = gate_len // 2
    last_tile = width // LANES - 1
    spare_chunk, spare_steps = chirp % gate_len // width, chirp // gate_len + 1
    halo_chunks = [(position // gate_len + 1, position % gate_len // width) for position in range(0, chirp, width)]
    edges = [[], [last_tile]]
    edges[spare_chunk] = [0] + edges[spare_chunk]

    rows = bins + TILE
    place = cut_places(place[0], place[1], rows)
    far_places = [exchanged(place, slot) for slot in cut_slots]
    place = place[:, None]
    sources = weight_tables(beam_weights, chirp)
    far_places = jnp.stack(
        [item for item in far_places for _ in range(beams)], axis=1
    )
    taps = toeplitz_taps(replica)
    first_blocks, far, far_edges, flag, weights = partial_beams(
        echoes, table, sources, beams, 0, width, edges[0], before=[taps, far_places]
    )
    fars, ends = [far], [far_edges]
    flag = passed_along(flag, "gate", 1)
    second_blocks, far, far_edges, _, _ = partial_beams(
        echoes, table, weights, beams, 1, width, edges[1], before=[flag]
    )
    fars, ends = fars + [far], ends + [far_edges]

    def with_halo(full, spare, left):
        before = passed_along(left, "gate", 1)
        after = [passed_along(full[chunk], "gate", -steps) for steps, chunk in halo_chunks]
        return [before] + full + after + [passed_along(spare, "gate", -spare_steps)]

    def neighbours(blocks):
        return [blocks[0]] + [
            exchanged(blocks[kind], whole_slots[kind]) for kind in range(1, len(whole_slots))
        ]

    first = summed_block(neighbours(first_blocks), edges[0])
    far_pieces = with_halo(fars, ends[spare_chunk][0], ends[1][-1])
    far_tiles = beam_tiles(taps, [(piece, 0) for piece in far_pieces], far_places, flag, gate_len)
    second = summed_block(neighbours(second_blocks), edges[1], before=[far_tiles])
    arrived = [
        exchanged(far_tiles[kind * beams : (kind + 1) * beams], slot)
        for kind, slot in enumerate(cut_slots)
    ]
    own_pieces = with_halo([first[0], second[0]], [first, second][spare_chunk][1], second[-1])
    results = []
    for beam in range(beams):
        tiles = beam_tiles(
            taps, [(piece, beam) for piece in own_pieces], place, flag, gate_len
        )
        tiles = slotted(
            [(tiles, 0)] + [(item, beam) for item in arrived], slots, owners * capacity
        )
        sent = lax.all_to_all(
            tiles.reshape(owners, capacity * 4, LANES),
            ("pulse", "gate"),
            split_axis=0,
            concat_axis=0,
            tiled=True,
        )
        results.append(sent.reshape(owners * capacity * 4, LANES))
    return finished(results, owners * capacity)


def solution(mesh):
    return jax.shard_map(
        local,
        mesh=mesh,
        in_specs=(
            P(None, None, "pulse", "gate"),
            P(),
            P(None, None, None, "pulse"),
            P(("pulse", "gate")),
            P(("pulse", "gate")),
            P(("pulse", "gate")),
        ),
        out_specs=P(("pulse", "gate"), None),
        check_vma=False,
    )
```

```python
import functools
import math

import jax
import jax.numpy as jnp
import ml_dtypes
import numpy as np
from jax import lax
from jax.experimental import pallas as pl
from jax.experimental.pallas import tpu as pltpu
from jax.sharding import PartitionSpec as P

TILE = 16
HALF = TILE // 2
LANES = 128
F32 = jnp.float32
BF16 = jnp.bfloat16
VMEM_LIMIT = 63 * 2**20
SMALL_COST = pl.CostEstimate(flops=2**20, bytes_accessed=2**16, transcendentals=0)


def passed_along(value, axis, steps):
    count = lax.axis_size(axis)
    leading, last = (max(0, -steps), min(count, count - steps))
    return lax.ppermute(value, axis, [(source, source + steps) for source in range(leading, last)])


def pulse_table(bins, depth):
    angle = 2.0 * np.pi * (np.outer(np.arange(bins), np.arange(depth)) % bins) / bins
    cos_part, sin_part = np.cos(angle), np.sin(angle)
    table = np.stack(
        [np.concatenate([cos_part, sin_part], 1), np.concatenate([-sin_part, cos_part], 1)]
    )
    table = table.reshape(2, bins // 8, 8, 2 * depth).transpose(1, 0, 2, 3)
    return table.reshape(2 * bins, 2 * depth).astype(ml_dtypes.bfloat16)


def gather_lines(me, parts, line_ref):
    count, bins = line_ref.shape[1], parts[0].shape[1]
    ends = jnp.zeros((HALF, count), F32)
    line_ref[:HALF, :] = ends
    line_ref[HALF + len(parts) * bins :, :] = ends
    for slot, part in enumerate(parts):
        first = pl.multiple_of((slot ^ me) * bins + HALF, 8)
        line_ref[pl.ds(first, bins), :] = part[:count, :].T


def quarter_turns(turn, ranks):
    cos_part = jnp.ones(turn.shape, F32)
    sin_part = jnp.zeros(turn.shape, F32)
    for value in range(1, ranks):
        angle = 2 * math.pi * value / ranks
        cos_part = jnp.where(turn == value, round(math.cos(angle), 12), cos_part)
        sin_part = jnp.where(turn == value, round(math.sin(angle), 12), sin_part)
    return cos_part, sin_part


def turn_tables(ranks, me, cos_ref, sin_ref, turned_ref):
    rows, lanes = cos_ref.shape
    offset = lax.broadcasted_iota(jnp.int32, (rows, lanes), 0) + (ranks * 8 - HALF)
    turn_cos, turn_sin = quarter_turns((me * offset) & (ranks - 1), ranks)
    base_cos, base_sin = cos_ref[...], sin_ref[...]
    turned_ref[0] = turn_cos * base_cos - turn_sin * base_sin
    turned_ref[1] = turn_sin * base_cos + turn_cos * base_sin


def fill_weights(ranks, bins, slot, me, line_ref, turned_ref, select_ref, weight_ref):
    groups, pairs, _, depth = weight_ref.shape
    per = divisor_up_to(groups, 11)
    span = per * 8
    lanes = turned_ref.shape[2]
    lane_id = lax.broadcasted_iota(jnp.int32, (8, lanes), 1)
    block = slot ^ me
    slot_cos, slot_sin = quarter_turns((block * (lane_id // 2 % ranks)) & (ranks - 1), ranks)
    first_part = lane_id[:1] % 2 == 0
    slot_cos, slot_sin = slot_cos[:1], slot_sin[:1]
    own_cos = jnp.where(first_part, slot_cos, slot_sin)
    own_sin = jnp.where(first_part, -slot_sin, slot_cos)
    cells = (span * 2, LANES)
    column = lax.broadcasted_iota(jnp.int32, cells, 1)
    diagonal = lax.broadcasted_iota(jnp.int32, cells, 0) % 8 == column % 8
    source_lane = column // 8
    for step in range(groups // per):
        here = slice(step * span, (step + 1) * span)
        rows = line_ref[pl.ds(pl.multiple_of(block * bins + step * span, 8), span), :]
        high = rows.astype(BF16)
        low = (rows - high.astype(F32)).astype(BF16)
        wide = jnp.dot(high, select_ref[...], preferred_element_type=F32) + jnp.dot(
            low, select_ref[...], preferred_element_type=F32
        )
        base_cos, base_sin = turned_ref[0, here, :], turned_ref[1, here, :]
        own = base_cos * own_cos + base_sin * own_sin
        other = base_sin * own_cos - base_cos * own_sin
        real, imag = wide[:, :lanes], wide[:, lanes:]
        out_real = (real * own + imag * other).reshape(per, 8, lanes)
        out_imag = (imag * own - real * other).reshape(per, 8, lanes)
        both = jnp.concatenate([out_real, out_imag], axis=1).reshape(span * 2, lanes)
        for first in range(0, lanes * 8, LANES):
            source = first // 8 // LANES * LANES
            wide = jnp.take_along_axis(
                both[:, source : source + LANES],
                source_lane + (first // 8 - source),
                axis=1,
                mode="promise_in_bounds",
            )
            wide = jnp.where(diagonal, wide, 0.0).astype(BF16).reshape(per, 16, LANES)
            lane = first % depth
            weight_ref[
                step * per : (step + 1) * per,
                first // depth * ranks + slot,
                :,
                lane : lane + LANES,
            ] = wide


def divisor_up_to(value, limit):
    return max(step for step in range(1, limit + 1) if value % step == 0)


def weight_tables(beam_weights, pulse_len):
    _, beams, channels, bins = beam_weights.shape
    ranks = lax.axis_size("pulse")
    total = bins * ranks
    count = 2 * beams * channels
    flat = beam_weights.reshape(count, bins)
    parts = [flat] + [
        lax.ppermute(flat, "pulse", [(rank, rank ^ slot) for rank in range(ranks)])
        for slot in range(1, ranks)
    ]
    small = channels * ranks * 2
    phase = np.arange(small) // 2 % ranks
    angle = 2.0 * np.pi * (np.outer(np.arange(bins + TILE) - HALF, phase) % total) / total
    scale = 1.0 / math.sqrt(total * 2.0 * pulse_len)
    base_cos = np.tile(np.cos(angle) * scale, (1, beams)).astype(np.float32)
    base_sin = np.tile(np.sin(angle) * scale, (1, beams)).astype(np.float32)
    target = np.arange(2 * beams * small)[None, :]
    wanted = target // small * channels + target % small // (2 * ranks)
    select = (np.arange(count)[:, None] == wanted).astype(ml_dtypes.bfloat16)
    me = lax.axis_index("pulse").reshape(1)
    return [me] + parts + [base_cos, base_sin, select]


def slot_kinds(ranks):
    whole_slots = [slot for slot in range(ranks) if slot & (slot - 1) == 0]
    return whole_slots, [slot for slot in range(ranks) if slot not in whole_slots]


def partial_beams_body(ranks, beams, edges, tables, before, echo_ref, table_ref, *rest):
    sources, rest = rest[: max(tables, 1)], rest[max(tables, 1) + before :]
    outs, (wide_ref, taken_ref, stage_ref, weight_ref, weight_sem) = rest[:-7], rest[-7:-2]
    line_ref, turned_ref = rest[-2:]
    whole_slots, cut_slots = slot_kinds(ranks)
    count = len(whole_slots)
    far_ref, edge_refs, flag_ref = outs[count], outs[count + 1 : count + 1 + len(edges)], outs[count + 1 + len(edges)]
    flag_ref[...] = jnp.ones(flag_ref.shape, F32)
    _, channels, pulses, width = echo_ref.shape
    depth = pulses // ranks
    groups = table_ref.shape[0] // 16
    columns = width // LANES
    turns = channels // 2
    if tables:
        me = sources[0][0]
        bins = sources[1].shape[1]
        gather_lines(me, sources[1 : 1 + ranks], line_ref)
        turn_tables(ranks, me, *sources[1 + ranks : 3 + ranks], turned_ref)

        def weights_of(slot):
            fill_weights(ranks, bins, slot, me, line_ref, turned_ref, sources[-1], weight_ref)

        if ranks % turns:
            lax.fori_loop(0, ranks, lambda slot, carry: (weights_of(slot), carry)[1], 0)
    else:
        fetch = pltpu.make_async_copy(sources[0], weight_ref, weight_sem)
        fetch.start()

    def deinterleave(channel, side):
        for part in range(2):
            wide = echo_ref[part, channel].astype(F32)
            for column in range(columns):
                wide_ref[side, part, column, :pulses] = wide[:, column * LANES : (column + 1) * LANES]
        for phase in range(ranks):
            here = pl.ds(phase, depth, stride=ranks)
            for part in range(2):
                for column in range(columns):
                    taken_ref[
                        side,
                        phase,
                        part * depth : (part + 1) * depth,
                        column * LANES : (column + 1) * LANES,
                    ] = wide_ref[side, part, column, here, :].astype(BF16)

    def transform(channel, side):
        for phase in range(ranks):
            product = jnp.dot(
                table_ref[...], taken_ref[side, phase], preferred_element_type=F32
            )
            stage_ref[:, channel * ranks + phase] = product.astype(BF16).reshape(groups, 16, width)

    deinterleave(0, 0)

    def two_channels(step, carry):
        first = step * 2
        deinterleave(first + 1, 1)
        transform(first, 0)
        deinterleave(lax.min(first + 2, channels - 1), 0)
        transform(first + 1, 1)
        if tables and ranks % turns == 0:
            for within in range(ranks // turns):
                weights_of(step * (ranks // turns) + within)
        return carry

    lax.fori_loop(0, turns, two_channels, 0)
    if tables:
        keep = pltpu.make_async_copy(weight_ref, outs[-1], weight_sem)
        keep.start()
    else:
        fetch.wait()

    _, pairs, _, inner = weight_ref.shape
    lines = pairs * 2
    steps = weight_ref.shape[0] // 2
    per = divisor_up_to(steps, 4)

    def combine(turn, carry):
        for within in range(per):
            step = turn * per + within
            halves = []
            for half in range(2):
                group = step * 2 + half
                source = lax.rem(group + groups - 1, groups)
                data = stage_ref[source].reshape(inner, width)
                weight = weight_ref[group].reshape(lines * 8, inner)
                product = jnp.dot(weight, data, preferred_element_type=F32)
                halves.append(product.reshape(lines, 8, width))
            both = jnp.concatenate(halves, axis=1).astype(BF16)
            here = pl.ds(pl.multiple_of(step * 16, 16), 16)
            for line in range(lines):
                beam, slot, part = line // (2 * ranks), line // 2 % ranks, line % 2
                value = both[line]
                for tile in range(columns):
                    piece = value[:, tile * LANES : (tile + 1) * LANES]
                    lanes = slice(part * LANES, (part + 1) * LANES)
                    if slot in whole_slots:
                        outs[whole_slots.index(slot)][beam, tile, here, lanes] = piece
                        continue
                    entry = cut_slots.index(slot) * beams + beam
                    far_ref[entry, tile, here, lanes] = piece
                    for edge, edge_ref in zip(edges, edge_refs):
                        if edge == tile:
                            edge_ref[entry, 0, here, lanes] = piece
        return carry

    lax.fori_loop(0, steps // per, combine, 0)
    if tables:
        keep.wait()


def partial_beams(echoes, table, sources, beams, chunk, width, edges, before=()):
    _, channels, pulses, _ = echoes.shape
    ranks = lax.axis_size("pulse")
    groups = table.shape[0] // 16
    rows = groups * 8 + TILE
    whole_slots, cut_slots = slot_kinds(ranks)
    far = len(cut_slots) * beams
    tiles = width // LANES
    tables = len(sources) if len(sources) > 1 else 0
    weights = jax.ShapeDtypeStruct((rows // 8, beams * ranks, 16, channels * ranks * 16), BF16)
    outs = [jax.ShapeDtypeStruct((beams, tiles, rows, 2 * LANES), BF16)] * len(whole_slots)
    outs += [jax.ShapeDtypeStruct((far, tiles, rows, 2 * LANES), BF16)]
    outs += [jax.ShapeDtypeStruct((far, 1, rows, 2 * LANES), BF16)] * len(edges)
    outs += [jax.ShapeDtypeStruct((8, LANES), F32)]
    whole = pl.BlockSpec(memory_space=pltpu.VMEM)
    anywhere = pl.BlockSpec(memory_space=pl.ANY)
    if tables:
        source_specs = [pl.BlockSpec(memory_space=pltpu.SMEM)] + [
            pl.BlockSpec(item.shape, lambda i: (0, 0)) for item in sources[1:]
        ]
    else:
        source_specs = [anywhere]
    result = pl.pallas_call(
        functools.partial(partial_beams_body, ranks, beams, edges, tables, len(before)),
        grid=(1,),
        out_shape=outs + ([weights] if tables else []),
        in_specs=[
            pl.BlockSpec((2, channels, pulses, width), lambda i: (0, 0, 0, chunk)),
            pl.BlockSpec(table.shape, lambda i: (0, 0)),
        ]
        + source_specs
        + [anywhere] * len(before),
        out_specs=[whole] * len(outs) + ([anywhere] if tables else []),
        scratch_shapes=[
            pltpu.VMEM((2, 2, width // LANES, pulses + 8, LANES), F32),
            pltpu.VMEM((2, ranks, 2 * pulses // ranks, width), BF16),
            pltpu.VMEM((groups, channels * ranks, 16, width), BF16),
            pltpu.VMEM(weights.shape, BF16),
            pltpu.SemaphoreType.DMA,
            pltpu.VMEM((ranks * groups * 8 + TILE, 2 * beams * channels), F32),
            pltpu.VMEM((2, rows, beams * channels * ranks * 2), F32),
        ],
        compiler_params=pltpu.CompilerParams(vmem_limit_bytes=VMEM_LIMIT),
        cost_estimate=SMALL_COST,
        name="partial_beams",
    )(echoes, table, *sources, *before)
    count = len(whole_slots)
    flag = count + 1 + len(edges)
    return result[:count], result[count], result[count + 1 : flag], result[flag], result[flag + 1 :]


def summed_body(terms, edges, *refs):
    ins, outs = refs[:terms], refs[-1 - len(edges) :]
    total = ins[0][...].astype(F32)
    for term in ins[1:]:
        total += term[...].astype(F32)
    total = total.astype(BF16)
    outs[0][...] = total
    for edge, edge_ref in zip(edges, outs[1:]):
        edge_ref[0, 0] = total[0, edge]


def summed_block(terms, edges, before=()):
    beams, tiles, rows, lanes = terms[0].shape
    block = pl.BlockSpec((1, tiles, rows, lanes), lambda i: (i, 0, 0, 0))
    single = pl.BlockSpec((1, 1, rows, lanes), lambda i: (i, 0, 0, 0))
    return pl.pallas_call(
        functools.partial(summed_body, len(terms), edges),
        grid=(beams,),
        out_shape=[jax.ShapeDtypeStruct(terms[0].shape, BF16)]
        + [jax.ShapeDtypeStruct((beams, 1, rows, lanes), BF16)] * len(edges),
        in_specs=[block] * len(terms) + [pl.BlockSpec(memory_space=pl.ANY)] * len(before),
        out_specs=[block] + [single] * len(edges),
        compiler_params=pltpu.CompilerParams(vmem_limit_bytes=VMEM_LIMIT),
        cost_estimate=SMALL_COST,
        name="summed_block",
    )(*terms, *before)


def toeplitz_body(replica_ref, out_ref):
    chirp = replica_ref.shape[1]
    span = chirp + LANES
    padded = jnp.concatenate(
        [replica_ref[...].astype(F32), jnp.zeros((2, LANES), F32)], axis=1
    )
    taps = []
    for part in range(2):
        rows = jnp.broadcast_to(padded[part : part + 1], (LANES, span))
        taps.append(pltpu.roll(rows, 0, 1, stride=1, stride_axis=0).T)
    real, imag = (tap.astype(BF16) for tap in taps)
    split = LANES // 2
    low, high = slice(0, split), slice(split, LANES)
    for part, (own, other) in enumerate(((real, -imag), (imag, real))):
        columns = jnp.concatenate(
            [own[:, low], other[:, low], other[:, high], own[:, high]], axis=1
        )
        for tile in range(span // LANES):
            first = (2 * tile + part) * LANES
            out_ref[first : first + LANES, :] = columns[tile * LANES : (tile + 1) * LANES]


def toeplitz_taps(replica):
    return pl.pallas_call(
        toeplitz_body,
        out_shape=jax.ShapeDtypeStruct((2 * (replica.shape[1] + LANES), 2 * LANES), BF16),
        cost_estimate=SMALL_COST,
        name="toeplitz_taps",
    )(replica)


def tiles_body(tracks, count, place_ref, flag_ref, taps_ref, repeat_ref, gather_ref, *rest):
    pieces, (out_ref, line_ref, cut_ref) = rest[:count], rest[-3:]
    entry = pl.program_id(0)
    rows = pieces[0].shape[2]
    span = taps_ref.shape[0] // (2 * LANES)
    columns = [(piece, tile) for piece in pieces for tile in range(piece.shape[1])]
    for block in range(len(columns) - span + 1):
        window = [piece[0, tile] for piece, tile in columns[block : block + span]]
        product = jnp.dot(
            jnp.concatenate(window, axis=1), taps_ref[...], preferred_element_type=F32
        )
        if block == 0:
            product = jnp.where(flag_ref[:1, :1] == 0.0, 0.0, product)
        line_ref[2 * block * rows : (2 * block + 1) * rows, :] = product[:, :LANES]
        line_ref[(2 * block + 1) * rows : (2 * block + 2) * rows, :] = product[:, LANES:]

    lane_id = lax.broadcasted_iota(jnp.int32, (TILE, LANES), 1) % (LANES // 2)
    batch = 16

    def cut(step, carry):
        values = []
        for within in range(batch):
            track = step * batch + within
            row = place_ref[0, entry, track]
            low = line_ref[pl.ds(row, TILE), :]
            high = line_ref[pl.ds(row + rows, TILE), :]
            values.append(jnp.where(lane_id >= place_ref[1, entry, track], low, high))
        values = [
            pltpu.roll(value, place_ref[2, entry, step * batch + within], 1)
            for within, value in enumerate(values)
        ]
        here = pl.ds(pl.multiple_of(step * batch * TILE, batch * TILE), batch * TILE)
        cut_ref[here, :] = jnp.concatenate(values, axis=0).astype(BF16)
        return carry

    lax.fori_loop(0, tracks // batch, cut, 0)

    group = 2 * LANES
    many = divisor_up_to(tracks * TILE // group, 4) * group
    row_id = lax.broadcasted_iota(jnp.int32, (many, group), 0) % 8
    wanted = row_id == lax.broadcasted_iota(jnp.int32, (many, group), 1) % LANES // TILE
    for start in range(0, tracks * TILE, many):
        repeated = jnp.dot(
            cut_ref[start : start + many, :], repeat_ref[...], preferred_element_type=F32
        )
        masked = jnp.where(wanted, repeated, 0.0).astype(BF16)
        for first in range(0, many, group):
            value = jnp.dot(
                gather_ref[...], masked[first : first + group], preferred_element_type=F32
            )
            here = (start + first) // 8
            out_ref[0, here : here + group // 8, :] = value.astype(BF16)


def slots_body(terms, slot_ref, *rest):
    parts, (out_ref, total_ref, sorted_ref) = rest[:terms], rest[-3:]
    total = parts[0][0].astype(F32)
    for part in parts[1:]:
        total += part[0].astype(F32)
    for part in range(2):
        total_ref[part] = total[:, part * LANES : (part + 1) * LANES]
    sorted_ref[...] = jnp.zeros(sorted_ref.shape, F32)

    def move(track, carry):
        target = pl.ds(slot_ref[track] * 2, 2)
        sorted_ref[:, target, :] = total_ref[:, pl.ds(track * 2, 2), :]
        return carry

    lax.fori_loop(0, slot_ref.shape[0], move, 0, unroll=8)
    for part in range(2):
        out_ref[:, part * LANES : (part + 1) * LANES] = sorted_ref[part].astype(BF16)


def slotted(terms, slots, slot_total):
    count, lanes = terms[0][0].shape[1:]
    return pl.pallas_call(
        functools.partial(slots_body, len(terms)),
        grid=(1,),
        out_shape=jax.ShapeDtypeStruct((slot_total * 2, lanes), BF16),
        in_specs=[pl.BlockSpec(memory_space=pltpu.SMEM)]
        + [
            pl.BlockSpec((1, count, lanes), lambda i, entry=entry: (entry, 0, 0))
            for _, entry in terms
        ],
        out_specs=pl.BlockSpec((slot_total * 2, lanes), lambda i: (0, 0)),
        scratch_shapes=[
            pltpu.VMEM((2, count, LANES), F32),
            pltpu.VMEM((2, slot_total * 2, LANES), F32),
        ],
        compiler_params=pltpu.CompilerParams(vmem_limit_bytes=VMEM_LIMIT),
        cost_estimate=SMALL_COST,
        name="slotted_tiles",
    )(slots, *[term for term, _ in terms])


def cut_places(bins, gates, rows):
    first = gates + (LANES - HALF)
    half = LANES // 2
    return jnp.stack([first // half * rows + bins, first % half, (LANES - first % LANES) % LANES])


def beam_tiles(taps, pieces, places, flag, gate_len):
    _, entries, tracks = places.shape
    rows = pieces[0][0].shape[2]
    scalar = pl.BlockSpec(memory_space=pltpu.SMEM)
    blocks = gate_len // LANES + 2
    group = 2 * LANES
    column = np.arange(group)[None, :]
    repeat = np.arange(LANES)[:, None] == column // LANES * (LANES // 2) + column % TILE
    repeat = repeat.astype(ml_dtypes.bfloat16)
    gather = np.arange(group // 8)[:, None] == np.arange(group)[None, :] // 8
    gather = gather.astype(ml_dtypes.bfloat16)
    return pl.pallas_call(
        functools.partial(tiles_body, tracks, len(pieces)),
        grid=(entries,),
        out_shape=jax.ShapeDtypeStruct((entries, tracks * 2, group), BF16),
        in_specs=[
            scalar,
            pl.BlockSpec(flag.shape, lambda i: (0, 0)),
            pl.BlockSpec(taps.shape, lambda i: (0, 0)),
            pl.BlockSpec(repeat.shape, lambda i: (0, 0)),
            pl.BlockSpec(gather.shape, lambda i: (0, 0)),
        ]
        + [
            pl.BlockSpec((1,) + piece.shape[1:], lambda i, offset=offset: (i + offset, 0, 0, 0))
            for piece, offset in pieces
        ],
        out_specs=pl.BlockSpec((1, tracks * 2, group), lambda i: (i, 0, 0)),
        scratch_shapes=[
            pltpu.VMEM((2 * blocks * rows, LANES), F32),
            pltpu.VMEM((tracks * TILE, LANES), BF16),
        ],
        compiler_params=pltpu.CompilerParams(vmem_limit_bytes=VMEM_LIMIT),
        cost_estimate=SMALL_COST,
        name="beam_tiles",
    )(places, flag, taps, repeat, gather, *[piece for piece, _ in pieces])


def finish_body(*refs):
    parts, out_ref, wide_ref = refs[:-2], refs[-2], refs[-1]
    rows = out_ref.shape[0]
    for beam, part in enumerate(parts):
        for side in range(2):
            wide_ref[: rows * 2] = part[:, side * LANES : (side + 1) * LANES].astype(F32)
            for half in range(2):
                column = ((side * len(parts) + beam) * 2 + half) * LANES
                out_ref[:, column : column + LANES] = wide_ref[pl.ds(half, rows, stride=2), :]


def finished(parts, rows):
    whole = pl.BlockSpec(memory_space=pltpu.VMEM)
    return pl.pallas_call(
        finish_body,
        out_shape=jax.ShapeDtypeStruct((rows, len(parts) * 4 * LANES), F32),
        in_specs=[whole] * len(parts),
        out_specs=whole,
        scratch_shapes=[pltpu.VMEM((rows * 2 + 8, LANES), F32)],
        compiler_params=pltpu.CompilerParams(vmem_limit_bytes=32 * 2**20),
        cost_estimate=SMALL_COST,
        name="finished_tiles",
    )(*parts)


def local(echoes, replica, beam_weights, track_doppler, track_gate, track_owner):
    gate_len = echoes.shape[3]
    chirp = replica.shape[1]
    _, beams, _, bins = beam_weights.shape
    ranks = lax.axis_size("pulse")
    owners = ranks * lax.axis_size("gate")
    table = pulse_table(bins, echoes.shape[2] // ranks)

    track_count = track_owner.shape[0]
    capacity = max(2, 5 * track_count // (2 * owners))
    owner_match = (
        track_owner[:, None] == jnp.arange(owners, dtype=jnp.int32)[None, :]
    ).astype(jnp.int32)
    running = jnp.cumsum(owner_match, axis=0, dtype=jnp.int32)
    slot_rank = jnp.sum(running * owner_match, axis=1, dtype=jnp.int32) - 1
    slots = track_owner * capacity + slot_rank
    place = jnp.stack([track_doppler % bins, track_gate % gate_len])

    def exchanged(value, slot):
        return lax.ppermute(value, "pulse", [(rank, rank ^ slot) for rank in range(ranks)])

    whole_slots, cut_slots = slot_kinds(ranks)

    width = gate_len // 2
    last_tile = width // LANES - 1
    spare_chunk, spare_steps = chirp % gate_len // width, chirp // gate_len + 1
    halo_chunks = [(position // gate_len + 1, position % gate_len // width) for position in range(0, chirp, width)]
    edges = [[], [last_tile]]
    edges[spare_chunk] = [0] + edges[spare_chunk]

    rows = bins + TILE
    place = cut_places(place[0], place[1], rows)
    far_places = [exchanged(place, slot) for slot in cut_slots]
    place = place[:, None]
    sources = weight_tables(beam_weights, chirp)
    far_places = jnp.stack(
        [item for item in far_places for _ in range(beams)], axis=1
    )
    taps = toeplitz_taps(replica)
    first_blocks, far, far_edges, flag, weights = partial_beams(
        echoes, table, sources, beams, 0, width, edges[0], before=[taps, far_places]
    )
    fars, ends = [far], [far_edges]
    flag = passed_along(flag, "gate", 1)
    second_blocks, far, far_edges, _, _ = partial_beams(
        echoes, table, weights, beams, 1, width, edges[1], before=[flag]
    )
    fars, ends = fars + [far], ends + [far_edges]

    def with_halo(full, spare, left):
        before = passed_along(left, "gate", 1)
        after = [passed_along(full[chunk], "gate", -steps) for steps, chunk in halo_chunks]
        return [before] + full + after + [passed_along(spare, "gate", -spare_steps)]

    def neighbours(blocks):
        return [blocks[0]] + [
            exchanged(blocks[kind], whole_slots[kind]) for kind in range(1, len(whole_slots))
        ]

    first = summed_block(neighbours(first_blocks), edges[0])
    far_pieces = with_halo(fars, ends[spare_chunk][0], ends[1][-1])
    far_tiles = beam_tiles(taps, [(piece, 0) for piece in far_pieces], far_places, flag, gate_len)
    second = summed_block(neighbours(second_blocks), edges[1], before=[far_tiles])
    arrived = [
        exchanged(far_tiles[kind * beams : (kind + 1) * beams], slot)
        for kind, slot in enumerate(cut_slots)
    ]
    own_pieces = with_halo([first[0], second[0]], [first, second][spare_chunk][1], second[-1])
    results = []
    for beam in range(beams):
        tiles = beam_tiles(
            taps, [(piece, beam) for piece in own_pieces], place, flag, gate_len
        )
        tiles = slotted(
            [(tiles, 0)] + [(item, beam) for item in arrived], slots, owners * capacity
        )
        sent = lax.all_to_all(
            tiles.reshape(owners, capacity * 2, 2 * LANES),
            ("pulse", "gate"),
            split_axis=0,
            concat_axis=0,
            tiled=True,
        )
        results.append(sent.reshape(owners * capacity * 2, 2 * LANES))
    return finished(results, owners * capacity)


def solution(mesh):
    return jax.shard_map(
        local,
        mesh=mesh,
        in_specs=(
            P(None, None, "pulse", "gate"),
            P(),
            P(None, None, None, "pulse"),
            P(("pulse", "gate")),
            P(("pulse", "gate")),
            P(("pulse", "gate")),
        ),
        out_specs=P(("pulse", "gate"), None),
        check_vma=False,
    )
```
